256 devices in a mesh: rep: 16 (over z_hi, y), zero: 16 (over z_lo, x, core).
Axes of the slice: x: 4, y: 4, z: 8 (z_hi: 4, z_lo: 2; z = z_hi * 2 + z_lo), core: 2. Of those that a mesh axis runs over, the one named last changes fastest.
Arguments:
- tokens: bfloat16 [256, 6144], P(None, 'zero'), may hold values from -6 to 6
- gate_weight: bfloat16 [6144, 14336], P('zero', 'rep'), may hold values from -0.078125 to 0.078125
- up_weight: bfloat16 [6144, 14336], P('zero', 'rep'), may hold values from -0.078125 to 0.078125
- down_weight: bfloat16 [14336, 6144], P('rep', 'zero'), may hold values from -0.046875 to 0.046875
- gate_scale: float32 [6144], P('zero'), may hold values from 0.5 to 2
- up_scale: float32 [6144], P('zero'), may hold values from 0.5 to 2
- down_scale: float32 [14336], P('rep'), may hold values from 0.5 to 2
- gate_probe: bfloat16 [6144, 14336], P('zero', 'rep'), may hold values from -1 to 1, as said below
- up_probe: bfloat16 [6144, 14336], P('zero', 'rep'), may hold values from -1 to 1, as said below
- down_probe: bfloat16 [14336, 6144], P('rep', 'zero'), may hold values from -1 to 1, as said below
Outputs:
- gate_gradient: float32 [6144, 14336], P('zero', 'rep')
- up_gradient: float32 [6144, 14336], P('zero', 'rep')
- down_gradient: float32 [14336, 6144], P('rep', 'zero')
- gate_hessian: float32 [6144, 14336], P('zero', 'rep')
- up_hessian: float32 [6144, 14336], P('zero', 'rep')
- down_hessian: float32 [14336, 6144], P('rep', 'zero')
The draws below stay inside these ranges and needn't reach their ends.
Inputs may be any that keep to these rules, and one draw needn't show every extreme that they name: `gate_probe`: every entry is +1 or -1. `up_probe`: every entry is +1 or -1. `down_probe`: every entry is +1 or -1.
All inputs are finite; a program needn't handle non-finite values.
Results may differ from the reference program's by a relative error of at most 0.0075.
Values may be sent and summed in bfloat16 or wider, within the bound.
A program may use at most 64 MiB of HBM per device.

```python
import math
import jax
import jax.numpy as jnp

D = 6144
H = 14336
TOKENS = 256


def draw_gate_probe(key, part):
    key = jax.random.fold_in(key, 11)
    signs = jax.random.bernoulli(key, 0.5, (D, H))
    return jnp.where(signs, 1.0, -1.0).astype(jnp.bfloat16)


def draw_up_probe(key, part):
    key = jax.random.fold_in(key, 12)
    signs = jax.random.bernoulli(key, 0.5, (D, H))
    return jnp.where(signs, 1.0, -1.0).astype(jnp.bfloat16)


def draw_down_probe(key, part):
    key = jax.random.fold_in(key, 13)
    signs = jax.random.bernoulli(key, 0.5, (H, D))
    return jnp.where(signs, 1.0, -1.0).astype(jnp.bfloat16)


def block_levels(own_key, dims, pieces, low, top_value):
    def one(position, blocks):
        draws = jax.random.uniform(jax.random.fold_in(jax.random.fold_in(own_key, 6), position), (blocks,), jnp.float32, low / len(pieces), top_value / len(pieces))
        return jnp.repeat(jnp.exp(draws), dims[position] // blocks).reshape((-1,) + (1,) * (len(dims) - position - 1))

    level = one(*pieces[0])
    for cut in pieces[1:]:
        level = level * one(*cut)
    return level


def centred(rng, shape, spread, bound, shards=(), held_as=jnp.bfloat16):
    gain = block_levels(rng, shape, shards, -0.22, 0.18) if shards else 1.0
    drawn = jax.random.normal(rng, shape, jnp.float32) * spread * gain
    return jnp.minimum(jnp.maximum(drawn, -bound), bound).astype(held_as)


def setup_inputs(seed: int = 0) -> dict:
    keys = jax.random.split(jax.random.key(seed), 11)
    return {
        "tokens": centred(keys[0], (TOKENS, D), 1.0, 6.0, ((1, 16),)),
        "gate_weight": centred(keys[1], (D, H), D ** -0.5, 0.078125, ((0, 16), (1, 16))),
        "up_weight": centred(keys[2], (D, H), D ** -0.5, 0.078125, ((0, 16), (1, 16))),
        "down_weight": centred(keys[3], (H, D), H ** -0.5, 0.046875, ((0, 16), (1, 16))),
        "gate_scale": jnp.clip(jnp.exp(math.log(2.0) - 1.3862944 * jax.random.uniform(keys[4], (D,), jnp.float32) ** block_levels(keys[4], (D,), ((0, 16),), -0.2, 0.2)), 0.5, 2.0),
        "up_scale": jnp.clip(jnp.exp(math.log(2.0) - 1.3862944 * jax.random.uniform(keys[5], (D,), jnp.float32) ** block_levels(keys[5], (D,), ((0, 16),), -0.2, 0.2)), 0.5, 2.0),
        "down_scale": jnp.clip(jnp.exp(math.log(2.0) - 1.3862944 * jax.random.uniform(keys[6], (H,), jnp.float32) ** block_levels(keys[6], (H,), ((0, 16),), -0.2, 0.2)), 0.5, 2.0),
        "gate_probe": draw_gate_probe(jax.random.fold_in(keys[10], 71), 0),
        "up_probe": draw_up_probe(jax.random.fold_in(keys[10], 71), 0),
        "down_probe": draw_down_probe(jax.random.fold_in(keys[10], 71), 0),
    }


def matmul(left, right):
    return jnp.dot(left, right, preferred_element_type=jnp.float32)


def dequantize(codes, scales):
    return (codes.astype(jnp.float32) * scales[:, None]).astype(jnp.bfloat16)


def silu_parts(gate_pre):
    logistic = jax.nn.sigmoid(gate_pre)
    activated = gate_pre * logistic
    slope = logistic * (1.0 + gate_pre * (1.0 - logistic))
    bend = logistic * (1.0 - logistic) * (2.0 + gate_pre * (1.0 - 2.0 * logistic))
    return activated, slope, bend


def reference(tokens, gate_weight, up_weight, down_weight, gate_scale, up_scale, down_scale, gate_probe, up_probe, down_probe):
    factor = float(TOKENS) ** -0.5
    feature_factor = float(D) ** -0.5
    hidden_factor = float(H) ** -0.5
    gate_matrix = dequantize(gate_weight, gate_scale)
    up_matrix = dequantize(up_weight, up_scale)
    down_matrix = dequantize(down_weight, down_scale)
    gate_pre = matmul(tokens, gate_matrix)
    up_pre = matmul(tokens, up_matrix)
    gate_tan = feature_factor * matmul(tokens, gate_probe)
    up_tan = feature_factor * matmul(tokens, up_probe)
    activated, slope, bend = silu_parts(gate_pre)
    hidden_act = (activated * up_pre).astype(jnp.bfloat16)
    tangent_act = (slope * gate_tan * up_pre + activated * up_tan).astype(jnp.bfloat16)
    output = matmul(hidden_act, down_matrix)
    output_tan = hidden_factor * matmul(hidden_act, down_probe) + matmul(tangent_act, down_matrix)
    back = (factor * (tokens.astype(jnp.float32) + output)).astype(jnp.bfloat16)
    back_tan = (factor * output_tan).astype(jnp.bfloat16)
    hid_back = matmul(back, down_matrix.T)
    hid_back_tan = matmul(back_tan, down_matrix.T) + hidden_factor * matmul(back, down_probe.T)
    gate_back = (hid_back * up_pre * slope).astype(jnp.bfloat16)
    up_back = (hid_back * activated).astype(jnp.bfloat16)
    gate_back_tan = (hid_back_tan * up_pre * slope + hid_back * (up_tan * slope + up_pre * bend * gate_tan)).astype(jnp.bfloat16)
    up_back_tan = (hid_back_tan * activated + hid_back * slope * gate_tan).astype(jnp.bfloat16)
    gate_gradient = matmul(tokens.T, gate_back)
    up_gradient = matmul(tokens.T, up_back)
    down_gradient = matmul(hidden_act.T, back)
    gate_hessian = matmul(tokens.T, gate_back_tan)
    up_hessian = matmul(tokens.T, up_back_tan)
    down_hessian = matmul(tangent_act.T, back) + matmul(hidden_act.T, back_tan)
    return (gate_gradient, up_gradient, down_gradient, gate_hessian, up_hessian, down_hessian)
```

```python
import functools

import jax
import jax.numpy as jnp
from jax import lax
from jax.experimental import pallas as pl
from jax.experimental.pallas import tpu as pltpu
from jax.sharding import PartitionSpec as P

D = 6144
H = 14336
TOKENS = 256

DL = 384
HL = 896
CHIPS = 8
REPS = 16
CHUNKS = 2
ROWS = 8

BF16 = jnp.bfloat16
F32 = jnp.float32
MESH = pl.DeviceIdType.MESH

ZERO_STEPS = tuple((dz, dx) for dz in range(2) for dx in range(4) if dz or dx)
REP_STEPS = tuple((dz, dy) for dz in range(4) for dy in range(4) if dz or dy)


def dot(left, right):
    return jnp.dot(left, right, preferred_element_type=F32)


def dot_last(left, right):
    return lax.dot_general(left, right, (((1,), (1,)), ((), ())), preferred_element_type=F32)


def dot_rows(left, right):
    return lax.dot_general(left, right, (((0,), (0,)), ((), ())), preferred_element_type=F32)


def pair(first, second):
    width = first.shape[-1]
    return jnp.concatenate([first.reshape(-1, ROWS, width), second.reshape(-1, ROWS, width)], axis=1).astype(BF16)


def exchange_kernel(
    tok_hbm, gw_hbm, uw_hbm, dw_hbm, gp_hbm, up_hbm, dp_hbm, gs_ref, us_ref, ds_ref,
    g_ref, x_ref, y_ref,
    tok, tok_sib, tok_order, gw, uw, gp, up, dw, dm, dp,
    sib_out, sib_in, own, stage, landed, mult,
    outs, outs_in, back, hid, hid_own, hid_in,
    load_sem, pre_s, pre_r, sib_s, sib_r, rs_s, rs_r, ag_s, ag_r, xs_s, xs_r,
    rep_s, rep_r, repag_s, repag_r, ys_s, ys_r, rs2_s, rs2_r, ag4_s, ag4_r, fw_s, fw_r,
):
    rep = lax.axis_index("rep")
    zero = lax.axis_index("zero")
    core = zero % 2
    chip = zero // 2
    z_lo, x = chip // 4, chip % 4
    z_hi, y = rep // 4, rep % 4
    sibling = (rep, chip * 2 + (1 - core))
    chips = [((z_lo + dz) % 2) * 4 + (x + dx) % 4 for dz, dx in ZERO_STEPS]
    chips_from = [((z_lo + dz) % 2) * 4 + (x + 4 - dx) % 4 for dz, dx in ZERO_STEPS]
    reps = [((z_hi + dz) % 4) * 4 + (y + dy) % 4 for dz, dy in REP_STEPS]

    def remote(src, dst, send, recv, device):
        return pltpu.make_async_remote_copy(
            src_ref=src, dst_ref=dst, send_sem=send, recv_sem=recv, device_id=device, device_id_type=MESH
        )

    barrier = pltpu.get_barrier_semaphore()
    pl.semaphore_signal(barrier, inc=1, device_id=sibling, device_id_type=MESH)
    for other in chips:
        pl.semaphore_signal(barrier, inc=1, device_id=(rep, other * 2 + core), device_id_type=MESH)
    for other in reps:
        pl.semaphore_signal(barrier, inc=1, device_id=(other, zero), device_id_type=MESH)

    loads = [
        pltpu.make_async_copy(src, dst, load_sem.at[n])
        for n, (src, dst) in enumerate(
            ((tok_hbm, tok), (gp_hbm, gp), (up_hbm, up), (gw_hbm, gw), (uw_hbm, uw), (dw_hbm, dw), (dp_hbm, dp.at[0]))
        )
    ]
    for copy in loads:
        copy.start()

    loads[0].wait()
    tok_order[0:128, :] = tok[pl.ds(pl.multiple_of((1 - core) * 128, 128), 128), :]
    tok_order[128:256, :] = tok[pl.ds(pl.multiple_of(core * 128, 128), 128), :]
    tokens = tok_order[...]

    def scaled(ref, scale_ref, out_ref, index=None):
        rows, width = ref.shape
        column = jnp.broadcast_to(scale_ref[...], (128, rows)).T
        for n in range(width // 128):
            block = (ref[:, n * 128 : (n + 1) * 128].astype(F32) * column).astype(BF16)
            if index is None:
                out_ref[:, n * 128 : (n + 1) * 128] = block
            else:
                out_ref[index, :, n * 128 : (n + 1) * 128] = block

    sib_copies = {}

    def pre(p, first, second):
        a = dot(tokens, first)
        b = dot(tokens, second)
        own[2 * p] = a[128:256]
        own[2 * p + 1] = b[128:256]
        both = pair(a[0:128], b[0:128])
        for q in range(CHUNKS):
            sib_out[q, p] = both[q * CHIPS : (q + 1) * CHIPS]
        for q in range(CHUNKS):
            copy = remote(sib_out.at[q, p], sib_in.at[q, p], sib_s.at[q, p], sib_r.at[q, p], sibling)
            sib_copies[q, p] = copy

    loads[1].wait()
    loads[2].wait()
    pre(0, gp[...], up[...])
    pl.semaphore_wait(barrier, 1 + len(chips) + len(reps))
    for q in range(CHUNKS):
        sib_copies[q, 0].start()
    loads[3].wait()
    scaled(gw, gs_ref, gw)
    loads[4].wait()
    scaled(uw, us_ref, uw)
    pre(1, gw[...], uw[...])
    for q in range(CHUNKS):
        sib_copies[q, 1].start()

    rs_copies = {}
    for q in range(CHUNKS):
        for p in range(2):
            sib_copies[q, p].wait_recv()
            a = own[2 * p, q * 64 : (q + 1) * 64].reshape(CHIPS, ROWS, HL)
            b = own[2 * p + 1, q * 64 : (q + 1) * 64].reshape(CHIPS, ROWS, HL)
            both = jnp.concatenate([a, b], axis=1) + sib_in[q, p].astype(F32)
            stage[q, :, p * 16 : (p + 1) * 16, :] = both.astype(BF16)
        for k, other in enumerate(chips):
            copy = remote(stage.at[q, other], landed.at[q, k], rs_s.at[q, k], rs_r.at[q, k], (rep, other * 2 + core))
            copy.start()
            rs_copies[q, k] = copy

    pre_copies = [
        remote(tok.at[pl.ds(pl.multiple_of((1 - core) * 128, 128), 128)], tok_sib, pre_s.at[0], pre_r.at[0], sibling)
    ]
    pre_copies[0].start()
    loads[5].wait()
    scaled(dw, ds_ref, dm, 0)
    loads[6].wait()
    pre_copies.append(remote(dm.at[0], dm.at[1], pre_s.at[1], pre_r.at[1], sibling))
    pre_copies.append(remote(dp.at[0], dp.at[1], pre_s.at[2], pre_r.at[2], sibling))
    pre_copies[1].start()
    pre_copies[2].start()

    feature_factor = float(D) ** -0.5
    hidden_factor = float(H) ** -0.5
    factor = float(TOKENS) ** -0.5

    ag_copies = {}
    for q in range(CHUNKS):
        row = pl.multiple_of(q * 64 + chip * ROWS, ROWS)
        total = [own[n, pl.ds(row, ROWS), :] for n in range(4)]
        for p in range(2):
            part = sib_in[q, p, chip].astype(F32)
            total[2 * p] += part[0:8]
            total[2 * p + 1] += part[8:16]
        for k in range(len(chips)):
            rs_copies[q, k].wait_recv()
            for p in range(2):
                part = landed[q, k, p * 16 : (p + 1) * 16, :].astype(F32)
                total[2 * p] += part[0:8]
                total[2 * p + 1] += part[8:16]
        gate_tan, up_tan, gate_pre, up_pre = total
        gate_tan = feature_factor * gate_tan
        up_tan = feature_factor * up_tan
        logistic = jax.nn.sigmoid(gate_pre)
        act = gate_pre * logistic
        slope = logistic * (1.0 + gate_pre * (1.0 - logistic))
        bend = logistic * (1.0 - logistic) * (2.0 + gate_pre * (1.0 - 2.0 * logistic))
        lean = slope * gate_tan
        x_ref[core, q, chip] = jnp.concatenate([act * up_pre, lean * up_pre + act * up_tan], axis=0).astype(BF16)
        for k, other in enumerate(chips):
            copy = remote(
                x_ref.at[core, q, chip], x_ref.at[core, q, chip], ag_s.at[q, k], ag_r.at[q, k], (rep, other * 2 + core)
            )
            copy.start()
            ag_copies[q, k] = copy
        mult[q, 0] = up_pre * slope
        mult[q, 1] = act
        mult[q, 2] = up_tan * slope + up_pre * bend * gate_tan
        mult[q, 3] = lean

    for copy in pre_copies:
        copy.wait_recv()
    xs_copies = []
    rep_copies = {}
    for q in range(CHUNKS):
        for k in range(len(chips)):
            ag_copies[q, k].wait_recv()
        copy = remote(x_ref.at[core, q], x_ref.at[core, q], xs_s.at[q], xs_r.at[q], sibling)
        copy.start()
        xs_copies.append(copy)
        hidden = x_ref[core, q].reshape(CHIPS * 16, HL)
        for f in range(2):
            straight = dot(hidden, dm[f]).reshape(CHIPS, 2, ROWS, DL)
            probed = dot(hidden, dp[f]).reshape(CHIPS, 2, ROWS, DL)
            outs[q, f] = jnp.concatenate(
                [straight[:, 0], hidden_factor * probed[:, 0] + straight[:, 1]], axis=1
            ).astype(BF16)
        for k, other in enumerate(reps):
            copy = remote(
                outs.at[q, other % 2, other // 2], outs_in.at[q, k], rep_s.at[q, k], rep_r.at[q, k], (other, zero)
            )
            copy.start()
            rep_copies[q, k] = copy

    group = rep // 2
    half = rep % 2
    repag_copies = {}
    for q in range(CHUNKS):
        total = outs[q, half, group].astype(F32)
        for k in range(len(reps)):
            rep_copies[q, k].wait_recv()
            total += outs_in[q, k].astype(F32)
        row = pl.multiple_of(q * 64 + (group // 2) * 16, 16)
        own_tokens = tok[pl.ds(pl.multiple_of(core * 128 + row, 16), 16), :].astype(F32)
        sib_tokens = tok_sib[pl.ds(row, 16), :].astype(F32)
        chosen = jnp.where(half == 0, own_tokens, sib_tokens)
        chosen = jnp.where(group % 2 == 0, chosen[0:8], chosen[8:16])
        back[q, half, group] = jnp.concatenate(
            [factor * (chosen + total[0:8]), factor * total[8:16]], axis=0
        ).astype(BF16)
        for k, other in enumerate(reps):
            copy = remote(
                back.at[q, half, group], back.at[q, half, group], repag_s.at[q, k], repag_r.at[q, k], (other, zero)
            )
            copy.start()
            repag_copies[q, k] = copy

    ys_copies = []
    rs2_copies = {}
    for q in range(CHUNKS):
        for k in range(len(reps)):
            repag_copies[q, k].wait_recv()
        copy = remote(back.at[q, 1], y_ref.at[core, q], ys_s.at[q], ys_r.at[q], sibling)
        copy.start()
        ys_copies.append(copy)
        signals = [back[q, f].reshape(CHIPS * 16, DL) for f in range(2)]
        straight = (dot_last(signals[0], dm[0]) + dot_last(signals[1], dm[1])).reshape(CHIPS, 2, ROWS, HL)
        probed = (dot_last(signals[0], dp[0]) + dot_last(signals[1], dp[1])).reshape(CHIPS, 2, ROWS, HL)
        both = jnp.concatenate([straight[:, 0], straight[:, 1] + hidden_factor * probed[:, 0]], axis=1)
        hid_own[...] = both
        hid[q] = both.astype(BF16)
        for k, other in enumerate(chips):
            copy = remote(hid.at[q, other], hid_in.at[q, k], rs2_s.at[q, k], rs2_r.at[q, k], (rep, other * 2 + core))
            copy.start()
            rs2_copies[q, k] = copy
        y_ref[core, q] = back[q, 0]

    ag4_copies = {}
    forwards = []
    for q in range(CHUNKS):
        total = hid[q, chip].astype(F32)
        for k in range(len(chips)):
            rs2_copies[q, k].wait_recv()
            total += hid_in[q, k].astype(F32)
        signal, signal_tan = total[0:8], total[8:16]
        gate_back = signal * mult[q, 0]
        up_back = signal * mult[q, 1]
        gate_back_tan = signal_tan * mult[q, 0] + signal * mult[q, 2]
        up_back_tan = signal_tan * mult[q, 1] + signal * mult[q, 3]
        g_ref[core, q, chip] = jnp.concatenate([gate_back, up_back, gate_back_tan, up_back_tan], axis=0).astype(BF16)
        for k, other in enumerate(chips):
            copy = remote(
                g_ref.at[core, q, chip], g_ref.at[core, q, chip], ag4_s.at[q, k], ag4_r.at[q, k],
                (rep, other * 2 + core),
            )
            copy.start()
            ag4_copies[q, k] = copy
        copy = remote(
            g_ref.at[core, q, chip], g_ref.at[core, q, chip], fw_s.at[q, 7], fw_r.at[q, 7], sibling
        )
        copy.start()
        forwards.append(copy)
    for q in range(CHUNKS):
        for k, origin in enumerate(chips_from):
            ag4_copies[q, k].wait_recv()
            copy = remote(
                g_ref.at[core, q, origin], g_ref.at[core, q, origin], fw_s.at[q, k], fw_r.at[q, k], sibling
            )
            copy.start()
            forwards.append(copy)

    for copies in (sib_copies, rs_copies, ag_copies, rep_copies, repag_copies, rs2_copies, ag4_copies):
        for copy in copies.values():
            copy.wait_send()
    for copy in pre_copies:
        copy.wait_send()
    for copies in (xs_copies, ys_copies, forwards):
        for copy in copies:
            copy.wait()


def exchange(*operands):
    vmem = pl.BlockSpec(memory_space=pltpu.VMEM)
    hbm = pl.BlockSpec(memory_space=pl.ANY)
    dma = pltpu.SemaphoreType.DMA
    peers, others = len(ZERO_STEPS), len(REP_STEPS)
    return pl.pallas_call(
        exchange_kernel,
        out_shape=(
            jax.ShapeDtypeStruct((2, CHUNKS, CHIPS, 32, HL), BF16),
            jax.ShapeDtypeStruct((2, CHUNKS, CHIPS, 16, HL), BF16),
            jax.ShapeDtypeStruct((2, CHUNKS, CHIPS, 16, DL), BF16),
        ),
        in_specs=[hbm] * 7 + [vmem] * 3,
        out_specs=(vmem, vmem, vmem),
        scratch_shapes=[
            pltpu.VMEM((256, DL), BF16),
            pltpu.VMEM((128, DL), BF16),
            pltpu.VMEM((256, DL), BF16),
            pltpu.VMEM((DL, HL), BF16),
            pltpu.VMEM((DL, HL), BF16),
            pltpu.VMEM((DL, HL), BF16),
            pltpu.VMEM((DL, HL), BF16),
            pltpu.VMEM((HL, DL), BF16),
            pltpu.VMEM((2, HL, DL), BF16),
            pltpu.VMEM((2, HL, DL), BF16),
            pltpu.VMEM((CHUNKS, 2, CHIPS, 16, HL), BF16),
            pltpu.VMEM((CHUNKS, 2, CHIPS, 16, HL), BF16),
            pltpu.VMEM((4, 128, HL), F32),
            pltpu.VMEM((CHUNKS, CHIPS, 32, HL), BF16),
            pltpu.VMEM((CHUNKS, peers, 32, HL), BF16),
            pltpu.VMEM((CHUNKS, 4, ROWS, HL), F32),
            pltpu.VMEM((CHUNKS, 2, CHIPS, 16, DL), BF16),
            pltpu.VMEM((CHUNKS, others, 16, DL), BF16),
            pltpu.VMEM((CHUNKS, 2, CHIPS, 16, DL), BF16),
            pltpu.VMEM((CHUNKS, CHIPS, 16, HL), BF16),
            pltpu.VMEM((CHIPS, 16, HL), F32),
            pltpu.VMEM((CHUNKS, peers, 16, HL), BF16),
            dma((7,)),
            dma((3,)), dma((3,)),
            dma((CHUNKS, 2)), dma((CHUNKS, 2)),
            dma((CHUNKS, peers)), dma((CHUNKS, peers)),
            dma((CHUNKS, peers)), dma((CHUNKS, peers)),
            dma((CHUNKS,)), dma((CHUNKS,)),
            dma((CHUNKS, others)), dma((CHUNKS, others)),
            dma((CHUNKS, others)), dma((CHUNKS, others)),
            dma((CHUNKS,)), dma((CHUNKS,)),
            dma((CHUNKS, peers)), dma((CHUNKS, peers)),
            dma((CHUNKS, peers)), dma((CHUNKS, peers)),
            dma((CHUNKS, peers + 1)), dma((CHUNKS, peers + 1)),
        ],
        compiler_params=pltpu.CompilerParams(
            collective_id=0, has_side_effects=True, vmem_limit_bytes=48 * 2**20
        ),
        name="exchange",
    )(*operands)


def products_kernel(tok, g, x, y, gg, ug, dg, gh, uh, dh, square, wide, sems):
    hidden = x[...].reshape(512, HL)
    signals = y[...].astype(F32).reshape(32, 2, ROWS, DL)
    straight = jnp.concatenate([signals[:, 0], jnp.zeros_like(signals[:, 0])], axis=1)
    swapped = jnp.concatenate([signals[:, 1], signals[:, 0]], axis=1)
    copies = []

    def put(buffer, n, out, sem):
        copy = pltpu.make_async_copy(buffer.at[n], out, sems.at[sem])
        copy.start()
        copies.append(copy)

    wide[0] = dot_rows(hidden, straight.astype(BF16).reshape(512, DL))
    put(wide, 0, dg, 0)
    wide[1] = dot_rows(hidden, swapped.astype(BF16).reshape(512, DL))
    put(wide, 1, dh, 1)
    tokens = tok[...]
    for n, out in enumerate((gg, ug, gh, uh)):
        part = g[:, :, :, (n // 2) * 16 : (n // 2) * 16 + 16, :].astype(F32).reshape(32, 2, ROWS, HL)
        rows = part[:, n % 2].reshape(256, HL).astype(BF16)
        square[n] = dot_rows(tokens, rows)
        put(square, n, out, 2 + n)
    for copy in copies:
        copy.wait()


def products(tok, g, x, y):
    vmem = pl.BlockSpec(memory_space=pltpu.VMEM)
    hbm = pl.BlockSpec(memory_space=pl.ANY)
    tall = jax.ShapeDtypeStruct((DL, HL), F32)
    flat = jax.ShapeDtypeStruct((HL, DL), F32)
    return pl.pallas_call(
        products_kernel,
        out_shape=(tall, tall, flat, tall, tall, flat),
        in_specs=[vmem] * 4,
        out_specs=[hbm] * 6,
        scratch_shapes=[
            pltpu.VMEM((4, DL, HL), F32),
            pltpu.VMEM((2, HL, DL), F32),
            pltpu.SemaphoreType.DMA((6,)),
        ],
        compiler_params=pltpu.CompilerParams(vmem_limit_bytes=48 * 2**20),
        name="products",
    )(tok, g, x, y)


def local(
    tokens, gate_weight, up_weight, down_weight, gate_scale, up_scale, down_scale, gate_probe, up_probe, down_probe
):
    g, x, y = exchange(
        tokens, gate_weight, up_weight, down_weight, gate_probe, up_probe, down_probe,
        gate_scale.reshape(1, DL), up_scale.reshape(1, DL), down_scale.reshape(1, HL),
    )
    return products(tokens, g, x, y)


def solution(mesh):
    in_specs = (
        P(None, "zero"),
        P("zero", "rep"),
        P("zero", "rep"),
        P("rep", "zero"),
        P("zero"),
        P("zero"),
        P("rep"),
        P("zero", "rep"),
        P("zero", "rep"),
        P("rep", "zero"),
    )
    out_specs = (
        P("zero", "rep"),
        P("zero", "rep"),
        P("rep", "zero"),
        P("zero", "rep"),
        P("zero", "rep"),
        P("rep", "zero"),
    )
    return jax.shard_map(local, mesh=mesh, in_specs=in_specs, out_specs=out_specs, check_vma=False)
```

```python
import functools

import jax
import jax.numpy as jnp
from jax import lax
from jax.experimental import pallas as pl
from jax.experimental.pallas import tpu as pltpu
from jax.sharding import PartitionSpec as P

D = 6144
H = 14336
TOKENS = 256

DL = 384
HL = 896
CHUNKS = 2
GROUPS = 8
ROWS = 8
BG = (1, 1, 0)
COPIES = 128

BF16 = jnp.bfloat16
F32 = jnp.float32
MESH = pl.DeviceIdType.MESH

ZERO_STEPS = ((1, 2), (1, 1), (1, 3), (0, 2), (1, 0), (0, 1), (0, 3))
RING_STEPS = (2, 1, 3)


def dot(left, right):
    return jnp.dot(left, right, preferred_element_type=F32)


def dot_last(left, right):
    return lax.dot_general(left, right, (((1,), (1,)), ((), ())), preferred_element_type=F32)


def dot_rows(left, right):
    return lax.dot_general(left, right, (((0,), (0,)), ((), ())), preferred_element_type=F32)


def pair(first, second):
    width = first.shape[-1]
    return jnp.concatenate([first.reshape(-1, ROWS, width), second.reshape(-1, ROWS, width)], axis=1).astype(BF16)


class Copies:
    def __init__(self, send, recv):
        self.send, self.recv = send, recv
        self.open = []

    def start(self, src, dst, device):
        n = len(self.open)
        copy = pltpu.make_async_remote_copy(
            src_ref=src, dst_ref=dst, send_sem=self.send.at[n], recv_sem=self.recv.at[n],
            device_id=device, device_id_type=MESH,
        )
        copy.start()
        entry = [copy, True]
        self.open.append(entry)
        return entry

    def arrive(self, *entries):
        for entry in entries:
            entry[0].wait_recv()
            entry[1] = False

    def finish(self):
        for copy, coming in self.open:
            copy.wait_send()
            if coming:
                copy.wait_recv()


def exchange_kernel(
    tok_hbm, gw_hbm, uw_hbm, dw_hbm, gp_hbm, up_hbm, dp_hbm, gs_hbm, us_hbm, ds_hbm,
    g_ref, dg_ref, dh_ref, turned,
    tok, tok_sib, tok_order, gw, uw, gp, up, dw, dm, dp, gs, us, ds,
    sib_out, sib_in, own, stage, far4, near4, sum4, mine4,
    x_ref, y_ref, hids, mult, outs, outs_in, mids, mids_in, back,
    hid, hid_in,
    load_sem, send_sem, recv_sem,
):
    rep = lax.axis_index("rep")
    zero = lax.axis_index("zero")
    core = zero % 2
    z_lo, x = zero // 8, (zero // 2) % 4
    z_hi, y = rep // 4, rep % 4
    sibling = (rep, zero + 1 - 2 * core)
    twin = (rep, (1 - z_lo) * 8 + x * 2 + core)
    xs = [(x + step) % 4 for step in RING_STEPS]
    ys = [(y + step) % 4 for step in RING_STEPS]
    zs = [(z_hi + step) % 4 for step in RING_STEPS]
    x_peers = [(rep, z_lo * 8 + other * 2 + core) for other in xs]
    y_peers = [(z_hi * 4 + other, zero) for other in ys]
    z_peers = [(other * 4 + y, zero) for other in zs]
    chips = [((x + dx) % 4, (z_lo + dz) % 2) for dz, dx in ZERO_STEPS]
    chips_from = [((x + 4 - dx) % 4, (z_lo + dz) % 2) for dz, dx in ZERO_STEPS]
    chip_peers = [(rep, other_z * 8 + other_x * 2 + core) for other_x, other_z in chips]
    partners = [sibling] + chip_peers + y_peers + z_peers
    copies = Copies(send_sem, recv_sem)

    barrier = pltpu.get_barrier_semaphore()
    for other in partners:
        pl.semaphore_signal(barrier, inc=1, device_id=other, device_id_type=MESH)

    pairs = (
        (tok_hbm, tok), (gp_hbm, gp), (up_hbm, up), (gs_hbm, gs), (gw_hbm, gw), (us_hbm, us), (uw_hbm, uw),
        (ds_hbm, ds), (dw_hbm, dw), (dp_hbm, dp.at[0]),
    )
    loads = [pltpu.make_async_copy(src, dst, load_sem.at[n]) for n, (src, dst) in enumerate(pairs)]
    for copy in loads:
        copy.start()

    loads[0].wait()
    tok_order[0:128, :] = tok[pl.ds(pl.multiple_of((1 - core) * 128, 128), 128), :]
    tok_order[128:256, :] = tok[pl.ds(pl.multiple_of(core * 128, 128), 128), :]
    tokens = tok_order[...]

    def scaled(ref, scale_ref, out_ref):
        rows, width = ref.shape
        column = jnp.broadcast_to(scale_ref[...].reshape(1, rows), (128, rows)).T
        for n in range(width // 128):
            block = slice(n * 128, (n + 1) * 128)
            out_ref[:, block] = (ref[:, block].astype(F32) * column).astype(BF16)

    from_sib = {}

    def pre(p, first, second):
        a = dot(tokens, first)
        b = dot(tokens, second)
        own[2 * p] = a[128:256]
        own[2 * p + 1] = b[128:256]
        both = pair(a[0:128], b[0:128])
        for q in range(CHUNKS):
            sib_out[q, p] = both[q * GROUPS : (q + 1) * GROUPS]

    def send_pre(p):
        for q in range(CHUNKS):
            from_sib[q, p] = copies.start(sib_out.at[q, p], sib_in.at[q, p], sibling)

    def sum_start(q, parts, far, near):
        if q == 0:
            return [copies.start(parts.at[other], far.at[k], x_peers[k]) for k, other in enumerate(xs)]
        return [copies.start(parts.at[:, 1 - z_lo], near, twin)]

    def sum_middle(q, parts, far, near, out, mine, ours, arrivals):
        if q == 0:
            total = ours
            for k, entry in enumerate(arrivals):
                copies.arrive(entry)
                total = total + far[k].astype(F32)
            mine[...] = jnp.where(z_lo == 0, total[0], total[1])
            out[0] = jnp.where(z_lo == 0, total[1], total[0]).astype(BF16)
            return [copies.start(out.at[0], near.at[0], twin)]
        copies.arrive(*arrivals)
        out[...] = (parts[:, z_lo].astype(F32) + near[...].astype(F32)).astype(BF16)
        entries = [copies.start(out.at[other], far.at[k, 0], x_peers[k]) for k, other in enumerate(xs)]
        mine[...] = ours + near[x].astype(F32)
        return entries

    def sum_end(q, far, near, mine, arrivals):
        copies.arrive(*arrivals)
        total = mine[...]
        if q == 0:
            return total + near[0].astype(F32)
        for k in range(3):
            total = total + far[k, 0].astype(F32)
        return total

    def gather(blocks):
        block = blocks.at[x, z_lo]
        return [copies.start(block, block, peer) for peer in chip_peers]

    feature_factor = float(D) ** -0.5
    hidden_factor = float(H) ** -0.5
    factor = float(TOKENS) ** -0.5

    def start_first(q):
        for p in range(2):
            copies.arrive(from_sib[q, p])
            a = own[2 * p, q * 64 : (q + 1) * 64].reshape(GROUPS, ROWS, HL)
            b = own[2 * p + 1, q * 64 : (q + 1) * 64].reshape(GROUPS, ROWS, HL)
            both = (jnp.concatenate([a, b], axis=1) + sib_in[q, p].astype(F32)).astype(BF16)
            stage[q, :, :, p * 16 : (p + 1) * 16, :] = both.reshape(4, 2, 16, HL)
        return sum_start(q, stage.at[q], far4.at[q], near4.at[q])

    def middle_first(q, arrivals):
        count = 2 if q == 0 else 1
        group = x * 2 if q == 0 else x * 2 + z_lo
        rows = pl.ds(pl.multiple_of(q * 64 + group * ROWS, ROWS), count * ROWS)
        kept = [own[n, rows, :].reshape(count, ROWS, HL) for n in range(4)]
        theirs = [sib_in[q, p, pl.ds(group, count)].astype(F32) for p in range(2)]
        ours = jnp.concatenate(kept, axis=1) + jnp.concatenate(theirs, axis=1)
        if q == 1:
            ours = ours[0]
        return sum_middle(q, stage.at[q], far4.at[q], near4.at[q], sum4.at[q], mine4.at[q], ours, arrivals)

    multipliers = []

    def activate(q, arrivals):
        total = sum_end(q, far4.at[q], near4.at[q], mine4.at[q], arrivals)
        gate_tan, up_tan, gate_pre, up_pre = [total[n * ROWS : (n + 1) * ROWS] for n in range(4)]
        gate_tan = feature_factor * gate_tan
        up_tan = feature_factor * up_tan
        logistic = jax.nn.sigmoid(gate_pre)
        act = gate_pre * logistic
        slope = logistic * (1.0 + gate_pre * (1.0 - logistic))
        bend = logistic * (1.0 - logistic) * (2.0 + gate_pre * (1.0 - 2.0 * logistic))
        lean = slope * gate_tan
        x_ref[core, q, x, z_lo] = jnp.concatenate([act * up_pre, lean * up_pre + act * up_tan], axis=0).astype(BF16)
        entries = gather(x_ref.at[core, q])
        mult[core, q, x, z_lo] = jnp.concatenate(
            [up_pre * slope, act, up_tan * slope + up_pre * bend * gate_tan, lean], axis=0
        ).astype(BF16)
        block = mult.at[core, q, x, z_lo]
        multipliers.append([copies.start(block, block, twin)])
        return entries

    waiting = list(range(CHUNKS))

    def background(count):
        for q in waiting[:count]:
            copies.arrive(*multipliers[q])
            block = mult.at[core, q, x]
            multipliers[q] = [copies.start(block, block, peer) for peer in x_peers]
        del waiting[:count]

    def share_multipliers(q):
        copies.arrive(*multipliers[q])
        return copies.start(mult.at[core, q], mult.at[core, q], sibling)

    def output(q, arrivals):
        copies.arrive(*arrivals)
        hidden = x_ref[core, q].reshape(GROUPS * 16, HL)
        for f in range(2):
            straight = dot(hidden, dm[f]).reshape(GROUPS, 2, ROWS, DL)
            probed = dot(hidden, dp[f]).reshape(GROUPS, 2, ROWS, DL)
            outs[q, f] = jnp.concatenate(
                [straight[:, 0], hidden_factor * probed[:, 0] + straight[:, 1]], axis=1
            ).astype(BF16).reshape(2, 4, 16, DL)
        entries = [
            copies.start(outs.at[q, other % 2, other // 2], outs_in.at[q, k], y_peers[k]) for k, other in enumerate(ys)
        ]
        return entries, copies.start(x_ref.at[core, q], x_ref.at[core, q], sibling)

    half, high = y % 2, y // 2

    def middle(q, arrivals):
        total = outs[q, half, high].astype(F32)
        for k, entry in enumerate(arrivals):
            copies.arrive(entry)
            total += outs_in[q, k].astype(F32)
        mids[q] = total.astype(BF16)
        return [copies.start(mids.at[q, other], mids_in.at[q, k], z_peers[k]) for k, other in enumerate(zs)]

    def cotangent(q, arrivals):
        total = mids[q, z_hi].astype(F32)
        for k, entry in enumerate(arrivals):
            copies.arrive(entry)
            total += mids_in[q, k].astype(F32)
        row = pl.multiple_of(q * 64 + high * 32 + (z_hi // 2) * 16, 16)
        own_tokens = tok[pl.ds(pl.multiple_of(core * 128 + row, 16), 16), :].astype(F32)
        sib_tokens = tok_sib[pl.ds(row, 16), :].astype(F32)
        chosen = jnp.where(half == 0, own_tokens, sib_tokens)
        chosen = jnp.where(z_hi % 2 == 0, chosen[0:8], chosen[8:16])
        back[q, half, high, z_hi] = jnp.concatenate(
            [factor * (chosen + total[0:8]), factor * total[8:16]], axis=0
        ).astype(BF16)
        block = back.at[q, half, high, z_hi]
        return [copies.start(block, block, peer) for peer in z_peers]

    def spread(q, arrivals):
        copies.arrive(*arrivals)
        block = back.at[q, half, high]
        return [copies.start(block, block, peer) for peer in y_peers]

    def backward(q, arrivals):
        copies.arrive(*arrivals)
        signals = [back[q, f].reshape(GROUPS * 16, DL) for f in range(2)]
        straight = (dot_last(signals[0], dm[0]) + dot_last(signals[1], dm[1])).reshape(GROUPS, 2, ROWS, HL)
        probed = (dot_last(signals[0], dp[0]) + dot_last(signals[1], dp[1])).reshape(GROUPS, 2, ROWS, HL)
        both = jnp.concatenate([straight[:, 0], straight[:, 1] + hidden_factor * probed[:, 0]], axis=1)
        hid[q] = both.astype(BF16).reshape(4, 2, 16, HL)
        entries = [copies.start(hid.at[q, *chip], hid_in.at[q, k], chip_peers[k]) for k, chip in enumerate(chips)]
        shared = copies.start(back.at[q, 1], y_ref.at[core, q], sibling)
        y_ref[core, q] = back[q, 0]
        return entries, shared

    def gradients(q, arrivals):
        total = hid[q, x, z_lo].astype(F32)
        for k, entry in enumerate(arrivals):
            copies.arrive(entry)
            total += hid_in[q, k].astype(F32)
        hids[core, q, x, z_lo] = total.astype(BF16)
        entries = gather(hids.at[core, q])
        block = hids.at[core, q, x, z_lo]
        return entries, copies.start(block, block, sibling)

    def combine(side, q, place_x, place_z):
        signals = hids[side, q, place_x, place_z].astype(F32)
        signal, signal_tan = signals[0:8], signals[8:16]
        factors = mult[side, q, place_x, place_z].astype(F32)
        first, second, third, fourth = [factors[n * ROWS : (n + 1) * ROWS] for n in range(4)]
        g_ref[side, q, place_x, place_z] = jnp.concatenate(
            [
                signal * first,
                signal * second,
                signal_tan * first + signal * third,
                signal_tan * second + signal * fourth,
            ],
            axis=0,
        ).astype(BF16)

    def down_products():
        hidden = x_ref[...].reshape(512, HL)
        signals = y_ref[...].astype(F32).reshape(32, 2, ROWS, DL)
        straight = jnp.concatenate([signals[:, 0], jnp.zeros_like(signals[:, 0])], axis=1)
        swapped = jnp.concatenate([signals[:, 1], signals[:, 0]], axis=1)
        dg_ref[...] = dot_rows(hidden, straight.astype(BF16).reshape(512, DL))
        dh_ref[...] = dot_rows(hidden, swapped.astype(BF16).reshape(512, DL))

    def prefetch():
        loads[7].wait()
        loads[8].wait()
        scaled(dw, ds, dm.at[0])
        loads[9].wait()
        theirs = tok.at[pl.ds(pl.multiple_of((1 - core) * 128, 128), 128)]
        return [
            copies.start(dm.at[0], dm.at[1], sibling),
            copies.start(dp.at[0], dp.at[1], sibling),
            copies.start(theirs, tok_sib, sibling),
        ]

    chunks = range(CHUNKS)
    loads[1].wait()
    loads[2].wait()
    pre(0, gp[...], up[...])
    pl.semaphore_wait(barrier, len(partners))
    send_pre(0)
    loads[3].wait()
    loads[4].wait()
    scaled(gw, gs, gw)
    loads[5].wait()
    loads[6].wait()
    scaled(uw, us, uw)
    pre(1, gw[...], uw[...])
    send_pre(1)
    flying = [start_first(q) for q in chunks]
    prefetched = prefetch()
    flying = [middle_first(q, flying[q]) for q in chunks]
    flying = [activate(q, flying[q]) for q in chunks]
    copies.arrive(*prefetched)
    shared = []
    flying, kept = zip(*[output(q, flying[q]) for q in chunks])
    shared += kept
    background(BG[0])
    turned[...] = tok[...].astype(F32).T.astype(BF16)
    flying = [middle(q, flying[q]) for q in chunks]
    background(BG[1])
    flying = [cotangent(q, flying[q]) for q in chunks]
    background(BG[2])
    flying = [spread(q, flying[q]) for q in chunks]
    flying, kept = zip(*[backward(q, flying[q]) for q in chunks])
    shared += kept
    shared += [share_multipliers(q) for q in chunks]
    flying, first = zip(*[gradients(q, flying[q]) for q in chunks])
    copies.arrive(*shared)
    for q in chunks:
        combine(core, q, x, z_lo)
    down_products()
    order = list(reversed(range(len(chips))))
    passed = []
    for q in chunks:
        for k in order:
            copies.arrive(flying[q][k])
            block = hids.at[core, q, *chips_from[k]]
            passed.append((q, k, copies.start(block, block, sibling)))
            combine(core, q, *chips_from[k])
    for q in chunks:
        copies.arrive(first[q])
        combine(1 - core, q, x, z_lo)
    for q, k, entry in passed:
        copies.arrive(entry)
        combine(1 - core, q, *chips_from[k])
    copies.finish()


def exchange(*operands):
    vmem = pl.BlockSpec(memory_space=pltpu.VMEM)
    hbm = pl.BlockSpec(memory_space=pltpu.HBM)
    return pl.pallas_call(
        exchange_kernel,
        out_shape=(
            pltpu.VMEM((2, CHUNKS, 4, 2, 32, HL), BF16),
            pltpu.VMEM((HL, DL), F32),
            pltpu.VMEM((HL, DL), F32),
            pltpu.VMEM((DL, 256), BF16),
        ),
        in_specs=[hbm] * 10,
        out_specs=(vmem, vmem, vmem, vmem),
        scratch_shapes=[
            pltpu.VMEM((256, DL), BF16),
            pltpu.VMEM((128, DL), BF16),
            pltpu.VMEM((256, DL), BF16),
            pltpu.VMEM((DL, HL), BF16),
            pltpu.VMEM((DL, HL), BF16),
            pltpu.VMEM((DL, HL), BF16),
            pltpu.VMEM((DL, HL), BF16),
            pltpu.VMEM((HL, DL), BF16),
            pltpu.VMEM((2, HL, DL), BF16),
            pltpu.VMEM((2, HL, DL), BF16),
            pltpu.VMEM((DL,), F32),
            pltpu.VMEM((DL,), F32),
            pltpu.VMEM((HL,), F32),
            pltpu.VMEM((CHUNKS, 2, GROUPS, 16, HL), BF16),
            pltpu.VMEM((CHUNKS, 2, GROUPS, 16, HL), BF16),
            pltpu.VMEM((4, 128, HL), F32),
            pltpu.VMEM((CHUNKS, 4, 2, 32, HL), BF16),
            pltpu.VMEM((CHUNKS, 3, 2, 32, HL), BF16),
            pltpu.VMEM((CHUNKS, 4, 32, HL), BF16),
            pltpu.VMEM((CHUNKS, 4, 32, HL), BF16),
            pltpu.VMEM((CHUNKS, 32, HL), F32),
            pltpu.VMEM((2, CHUNKS, 4, 2, 16, HL), BF16),
            pltpu.VMEM((2, CHUNKS, 2, 4, 16, DL), BF16),
            pltpu.VMEM((2, CHUNKS, 4, 2, 16, HL), BF16),
            pltpu.VMEM((2, CHUNKS, 4, 2, 32, HL), BF16),
            pltpu.VMEM((CHUNKS, 2, 2, 4, 16, DL), BF16),
            pltpu.VMEM((CHUNKS, 3, 4, 16, DL), BF16),
            pltpu.VMEM((CHUNKS, 4, 16, DL), BF16),
            pltpu.VMEM((CHUNKS, 3, 16, DL), BF16),
            pltpu.VMEM((CHUNKS, 2, 2, 4, 16, DL), BF16),
            pltpu.VMEM((CHUNKS, 4, 2, 16, HL), BF16),
            pltpu.VMEM((CHUNKS, len(ZERO_STEPS), 16, HL), BF16),
            pltpu.SemaphoreType.DMA((10,)),
            pltpu.SemaphoreType.DMA((COPIES,)),
            pltpu.SemaphoreType.DMA((COPIES,)),
        ],
        compiler_params=pltpu.CompilerParams(
            collective_id=0, has_side_effects=True, vmem_limit_bytes=44 * 2**20
        ),
        name="exchange",
    )(*[pltpu.with_memory_space_constraint(operand, pltpu.HBM) for operand in operands])


def products_kernel(turned, g, down, down_tan, gg, ug, dg, gh, uh, dh, square, sems):
    copies = []

    def put(src, out, sem):
        copy = pltpu.make_async_copy(src, out, sems.at[sem])
        copy.start()
        copies.append(copy)

    put(down, dg, 0)
    put(down_tan, dh, 1)
    tokens = turned[...]
    for n, out in enumerate((gg, ug, gh, uh)):
        part = g[:, :, :, :, (n // 2) * 16 : (n // 2) * 16 + 16, :].astype(F32).reshape(32, 2, ROWS, HL)
        rows = part[:, n % 2].reshape(256, HL).astype(BF16)
        square[n] = dot(tokens, rows)
        put(square.at[n], out, 2 + n)
    for copy in copies:
        copy.wait()


def products(turned, g, down, down_tan):
    vmem = pl.BlockSpec(memory_space=pltpu.VMEM)
    hbm = pl.BlockSpec(memory_space=pl.ANY)
    tall = jax.ShapeDtypeStruct((DL, HL), F32)
    flat = jax.ShapeDtypeStruct((HL, DL), F32)
    return pl.pallas_call(
        products_kernel,
        out_shape=(tall, tall, flat, tall, tall, flat),
        in_specs=[vmem] * 4,
        out_specs=[hbm] * 6,
        scratch_shapes=[pltpu.VMEM((4, DL, HL), F32), pltpu.SemaphoreType.DMA((6,))],
        compiler_params=pltpu.CompilerParams(vmem_limit_bytes=40 * 2**20),
        name="products",
    )(turned, g, down, down_tan)


def local(
    tokens, gate_weight, up_weight, down_weight, gate_scale, up_scale, down_scale, gate_probe, up_probe, down_probe
):
    g, down, down_tan, turned = exchange(
        tokens, gate_weight, up_weight, down_weight, gate_probe, up_probe, down_probe,
        gate_scale, up_scale, down_scale,
    )
    return products(turned, g, down, down_tan)


def solution(mesh):
    in_specs = (
        P(None, "zero"),
        P("zero", "rep"),
        P("zero", "rep"),
        P("rep", "zero"),
        P("zero"),
        P("zero"),
        P("rep"),
        P("zero", "rep"),
        P("zero", "rep"),
        P("rep", "zero"),
    )
    out_specs = (
        P("zero", "rep"),
        P("zero", "rep"),
        P("rep", "zero"),
        P("zero", "rep"),
        P("zero", "rep"),
        P("rep", "zero"),
    )
    return jax.shard_map(local, mesh=mesh, in_specs=in_specs, out_specs=out_specs, check_vma=False)
```

```python
import functools

import jax
import jax.numpy as jnp
from jax import lax
from jax.experimental import pallas as pl
from jax.experimental.pallas import tpu as pltpu
from jax.sharding import PartitionSpec as P

D = 6144
H = 14336
TOKENS = 256

DL = 384
HL = 896
CHUNKS = 2
GROUPS = 8
ROWS = 8
BACKGROUND = (1, 1, 0)
GROUPS_SENT = 45
SENDS = 12

BF16 = jnp.bfloat16
F32 = jnp.float32
MESH = pl.DeviceIdType.MESH

ZERO_STEPS = ((1, 2), (1, 1), (1, 3), (0, 2), (1, 0), (0, 1), (0, 3))
RING_STEPS = (2, 1, 3)


def dot(left, right):
    return jnp.dot(left, right, preferred_element_type=F32)


def dot_last(left, right):
    return lax.dot_general(left, right, (((1,), (1,)), ((), ())), preferred_element_type=F32)


def dot_rows(left, right):
    return lax.dot_general(left, right, (((0,), (0,)), ((), ())), preferred_element_type=F32)


def pair(first, second):
    width = first.shape[-1]
    return jnp.concatenate([first.reshape(-1, ROWS, width), second.reshape(-1, ROWS, width)], axis=1).astype(BF16)


class Copies:
    def __init__(self, send, recv, device):
        self.send, self.recv, self.device = send, recv, device
        self.groups = []
        self.busy = {}

    def start(self, moves, view):
        n = len(self.groups)
        slot = n % SENDS
        if slot in self.busy:
            self.busy.pop(slot).wait_send()
        for src, dst, device in moves:
            pltpu.make_async_remote_copy(
                src_ref=src, dst_ref=dst, send_sem=self.send.at[slot], recv_sem=self.recv.at[n],
                device_id=device, device_id_type=MESH,
            ).start()
        group = pltpu.make_async_remote_copy(
            src_ref=view, dst_ref=view, send_sem=self.send.at[slot], recv_sem=self.recv.at[n],
            device_id=self.device, device_id_type=MESH,
        )
        self.busy[slot] = group
        self.groups.append(group)
        return group

    def one(self, src, dst, device):
        return self.start([(src, dst, device)], dst)

    def arrive(self, *groups):
        for group in groups:
            group.wait_recv()

    def sent(self):
        for slot in list(self.busy):
            self.busy.pop(slot).wait_send()


def exchange_kernel(
    tok_hbm, gw_hbm, uw_hbm, dw_hbm, gp_hbm, up_hbm, dp_hbm, gs_hbm, us_hbm, ds_hbm,
    g_ref, dg_ref, dh_ref, turned,
    tok, tok_sib, tok_order, mats, dw, wide, gs, us, ds,
    sib_out, sib_in, own, stage, far4, near4, sum4, mine4,
    x_ref, y_ref, hids, mult, outs, outs_in, mids, mids_in, back,
    hid, hid_in,
    load_sem, send_sem, recv_sem,
):
    rep = lax.axis_index("rep")
    zero = lax.axis_index("zero")
    core = lax.rem(zero, 2)
    z_lo, x = lax.div(zero, 8), lax.rem(lax.div(zero, 2), 4)
    z_hi, y = lax.div(rep, 4), lax.rem(rep, 4)
    sibling = (rep, zero + 1 - 2 * core)
    twin = (rep, (1 - z_lo) * 8 + x * 2 + core)
    ring_x = [x] + [lax.rem(x + step, 4) for step in (1, 2, 3)]
    xs = [ring_x[step] for step in RING_STEPS]
    ys = [lax.rem(y + step, 4) for step in RING_STEPS]
    zs = [lax.rem(z_hi + step, 4) for step in RING_STEPS]
    x_peers = [(rep, z_lo * 8 + other * 2 + core) for other in xs]
    y_peers = [(z_hi * 4 + other, zero) for other in ys]
    z_peers = [(other * 4 + y, zero) for other in zs]
    ring_z = [z_lo, 1 - z_lo]
    chips = [(ring_x[dx], ring_z[dz]) for dz, dx in ZERO_STEPS]
    chips_from = [(ring_x[(4 - dx) % 4], ring_z[dz]) for dz, dx in ZERO_STEPS]
    places = [2 * other_x + other_z for other_x, other_z in chips]
    places_from = [2 * other_x + other_z for other_x, other_z in chips_from]
    chip_peers = [(rep, other_z * 8 + other_x * 2 + core) for other_x, other_z in chips]
    partners = [sibling] + chip_peers + y_peers + z_peers
    copies = Copies(send_sem, recv_sem, sibling)

    barrier = pltpu.get_barrier_semaphore()
    for other in partners:
        pl.semaphore_signal(barrier, inc=1, device_id=other, device_id_type=MESH)

    gp, up = mats.at[0, :, pl.ds(0, HL)], mats.at[0, :, pl.ds(HL, HL)]
    gw, uw = mats.at[1, :, pl.ds(0, HL)], mats.at[1, :, pl.ds(HL, HL)]
    pairs = (
        (tok_hbm, tok), (gp_hbm, gp), (up_hbm, up), (gs_hbm, gs), (gw_hbm, gw), (us_hbm, us), (uw_hbm, uw),
        (ds_hbm, ds), (dw_hbm, dw), (dp_hbm, wide.at[:, pl.ds(2 * DL, DL)]),
    )
    loads = [pltpu.make_async_copy(src, dst, load_sem.at[n]) for n, (src, dst) in enumerate(pairs)]
    for copy in loads:
        copy.start()

    loads[0].wait()
    tok_order[0:128, :] = tok[pl.ds(pl.multiple_of((1 - core) * 128, 128), 128), :]
    tok_order[128:256, :] = tok[pl.ds(pl.multiple_of(core * 128, 128), 128), :]
    tokens = tok_order[...]

    def scaled(ref, scale_ref, out_ref, rows, width):
        column = jnp.broadcast_to(scale_ref[...].reshape(1, rows), (128, rows)).T
        for n in range(width // 128):
            block = slice(n * 128, (n + 1) * 128)
            out_ref[:, block] = (ref[:, block].astype(F32) * column).astype(BF16)

    from_sib = {}

    def pre(p):
        wide_result = dot(tokens, mats[p])
        a, b = wide_result[:, 0:HL], wide_result[:, HL : 2 * HL]
        own[2 * p] = a[128:256]
        own[2 * p + 1] = b[128:256]
        both = pair(a[0:128], b[0:128])
        for q in range(CHUNKS):
            sib_out[q, p] = both[q * GROUPS : (q + 1) * GROUPS]

    def send_pre(p):
        for q in range(CHUNKS):
            from_sib[q, p] = copies.one(sib_out.at[q, p], sib_in.at[q, p], sibling)

    def sum_start(q, parts, far, near):
        if q == 0:
            return copies.start([(parts.at[other], far.at[k], x_peers[k]) for k, other in enumerate(xs)], far)
        return copies.one(parts.at[:, 1 - z_lo], near, twin)

    def sum_middle(q, parts, far, near, out, mine, ours, arrival):
        copies.arrive(arrival)
        if q == 0:
            total = ours
            for k in range(3):
                total = total + far[k].astype(F32)
            mine[...] = jnp.where(z_lo == 0, total[0], total[1])
            out[0] = jnp.where(z_lo == 0, total[1], total[0]).astype(BF16)
            return copies.one(out.at[0], near.at[0], twin)
        out[...] = (parts[:, z_lo].astype(F32) + near[...].astype(F32)).astype(BF16)
        group = copies.start(
            [(out.at[other], far.at[k, 0], x_peers[k]) for k, other in enumerate(xs)], far.at[:, 0]
        )
        mine[...] = ours + near[x].astype(F32)
        return group

    def sum_end(q, far, near, mine, arrival):
        copies.arrive(arrival)
        total = mine[...]
        if q == 0:
            return total + near[0].astype(F32)
        for k in range(3):
            total = total + far[k, 0].astype(F32)
        return total

    place = 2 * x + z_lo

    def gather(blocks, steps):
        block = blocks.at[place]
        return copies.start([(block, block, chip_peers[k]) for k in steps], blocks.at[pl.ds(0, len(steps))])

    feature_factor = float(D) ** -0.5
    hidden_factor = float(H) ** -0.5
    factor = float(TOKENS) ** -0.5

    def start_first(q, p):
        copies.arrive(from_sib[q, p])
        a = own[2 * p, q * 64 : (q + 1) * 64].reshape(GROUPS, ROWS, HL)
        b = own[2 * p + 1, q * 64 : (q + 1) * 64].reshape(GROUPS, ROWS, HL)
        both = (jnp.concatenate([a, b], axis=1) + sib_in[q, p].astype(F32)).astype(BF16)
        stage[q, p] = both.reshape(4, 2, 16, HL)
        return sum_start(q, stage.at[q, p], far4.at[q, p], near4.at[q, p])

    def middle_first(q, p, arrivals):
        count = 2 if q == 0 else 1
        group = x * 2 if q == 0 else x * 2 + z_lo
        rows = pl.ds(pl.multiple_of(q * 64 + group * ROWS, ROWS), count * ROWS)
        kept = [own[2 * p + n, rows, :].reshape(count, ROWS, HL) for n in range(2)]
        ours = jnp.concatenate(kept, axis=1) + sib_in[q, p, pl.ds(group, count)].astype(F32)
        if q == 1:
            ours = ours[0]
        return sum_middle(
            q, stage.at[q, p], far4.at[q, p], near4.at[q, p], sum4.at[q, p], mine4.at[q, p], ours, arrivals
        )

    multipliers = []

    def activate(q, arrivals):
        totals = [
            sum_end(q, far4.at[q, p], near4.at[q, p], mine4.at[q, p], arrivals[p]) for p in range(2)
        ]
        gate_tan, up_tan, gate_pre, up_pre = [total[n : n + ROWS] for total in totals for n in (0, ROWS)]
        gate_tan = feature_factor * gate_tan
        up_tan = feature_factor * up_tan
        logistic = jax.nn.sigmoid(gate_pre)
        act = gate_pre * logistic
        slope = logistic * (1.0 + gate_pre * (1.0 - logistic))
        bend = logistic * (1.0 - logistic) * (2.0 + gate_pre * (1.0 - 2.0 * logistic))
        lean = slope * gate_tan
        x_ref[core, q, place] = jnp.concatenate([act * up_pre, lean * up_pre + act * up_tan], axis=0).astype(BF16)
        group = gather(x_ref.at[core, q], range(len(chips)))
        mult[core, q, place] = jnp.concatenate(
            [up_pre * slope, act, up_tan * slope + up_pre * bend * gate_tan, lean], axis=0
        ).astype(BF16)
        block = mult.at[core, q, place]
        multipliers.append(copies.one(block, block, twin))
        return group

    waiting = list(range(CHUNKS))

    def background(count):
        for q in waiting[:count]:
            copies.arrive(multipliers[q])
            block = mult.at[core, q, pl.ds(2 * x, 2)]
            multipliers[q] = copies.start([(block, block, peer) for peer in x_peers], mult.at[core, q, pl.ds(0, 6)])
        del waiting[:count]

    def share_multipliers(q):
        copies.arrive(multipliers[q])
        return copies.one(mult.at[core, q], mult.at[core, q], sibling)

    def output(q, arrival):
        copies.arrive(arrival)
        hidden = x_ref[core, q].reshape(GROUPS * 16, HL)
        result = dot(hidden, wide[...])
        for f in range(2):
            straight = result[:, f * DL : (f + 1) * DL].reshape(GROUPS, 2, ROWS, DL)
            probed = result[:, (f + 2) * DL : (f + 3) * DL].reshape(GROUPS, 2, ROWS, DL)
            outs[q, f] = jnp.concatenate(
                [straight[:, 0], hidden_factor * probed[:, 0] + straight[:, 1]], axis=1
            ).astype(BF16).reshape(2, 4, 16, DL)
        group = copies.start(
            [(outs.at[q, lax.rem(other, 2), lax.div(other, 2)], outs_in.at[q, k], y_peers[k]) for k, other in enumerate(ys)],
            outs_in.at[q],
        )
        return group, copies.one(x_ref.at[core, q], x_ref.at[core, q], sibling)

    half, high = lax.rem(y, 2), lax.div(y, 2)

    def middle(q, arrival):
        copies.arrive(arrival)
        total = outs[q, half, high].astype(F32)
        for k in range(3):
            total += outs_in[q, k].astype(F32)
        mids[q] = total.astype(BF16)
        return copies.start(
            [(mids.at[q, other], mids_in.at[q, k], z_peers[k]) for k, other in enumerate(zs)], mids_in.at[q]
        )

    def cotangent(q, arrival):
        copies.arrive(arrival)
        total = mids[q, z_hi].astype(F32)
        for k in range(3):
            total += mids_in[q, k].astype(F32)
        row = pl.multiple_of(q * 64 + high * 32 + lax.div(z_hi, 2) * 16, 16)
        own_tokens = tok[pl.ds(pl.multiple_of(core * 128 + row, 16), 16), :].astype(F32)
        sib_tokens = tok_sib[pl.ds(row, 16), :].astype(F32)
        chosen = jnp.where(half == 0, own_tokens, sib_tokens)
        chosen = jnp.where(lax.rem(z_hi, 2) == 0, chosen[0:8], chosen[8:16])
        back[q, half, high, z_hi] = jnp.concatenate(
            [factor * (chosen + total[0:8]), factor * total[8:16]], axis=0
        ).astype(BF16)
        block = back.at[q, half, high, z_hi]
        return copies.start([(block, block, peer) for peer in z_peers], back.at[q, half, high, pl.ds(0, 3)])

    def spread(q, arrival):
        copies.arrive(arrival)
        block = back.at[q, half, high]
        return copies.start([(block, block, peer) for peer in y_peers], outs_in.at[q])

    def backward(q, arrival):
        copies.arrive(arrival)
        signals = jnp.concatenate([back[q, f].reshape(GROUPS * 16, DL) for f in range(2)], axis=1)
        straight = dot_last(signals, wide[:, 0 : 2 * DL]).reshape(GROUPS, 2, ROWS, HL)
        probed = dot_last(signals, wide[:, 2 * DL : 4 * DL]).reshape(GROUPS, 2, ROWS, HL)
        both = jnp.concatenate([straight[:, 0], straight[:, 1] + hidden_factor * probed[:, 0]], axis=1)
        hid[q] = both.astype(BF16)
        group = copies.start(
            [(hid.at[q, other], hid_in.at[q, k], chip_peers[k]) for k, other in enumerate(places)], hid_in.at[q]
        )
        shared = copies.one(back.at[q, 1], y_ref.at[core, q], sibling)
        y_ref[core, q] = back[q, 0]
        return group, shared

    parts = (range(0, 4), range(4, 7))

    def pass_on(q, origins):
        blocks = [hids.at[core, q, n] for n in origins]
        return copies.start([(block, block, sibling) for block in blocks], hids.at[core, q, pl.ds(0, len(blocks))])

    def gradients(q, arrival):
        copies.arrive(arrival)
        total = hid[q, place].astype(F32)
        for k in range(len(chips)):
            total += hid_in[q, k].astype(F32)
        hids[core, q, place] = total.astype(BF16)
        return [gather(hids.at[core, q], steps) for steps in parts]

    def combine(side, q, n):
        signals = hids[side, q, n].astype(F32)
        signal, signal_tan = signals[0:8], signals[8:16]
        factors = mult[side, q, n].astype(F32)
        first, second, third, fourth = [factors[m * ROWS : (m + 1) * ROWS] for m in range(4)]
        g_ref[side, q, n] = jnp.concatenate(
            [
                signal * first,
                signal * second,
                signal_tan * first + signal * third,
                signal_tan * second + signal * fourth,
            ],
            axis=0,
        ).astype(BF16)

    def down_products():
        hidden = x_ref[...].reshape(512, HL)
        signals = y_ref[...].astype(F32).reshape(32, 2, ROWS, DL)
        straight = jnp.concatenate([signals[:, 0], jnp.zeros_like(signals[:, 0])], axis=1)
        swapped = jnp.concatenate([signals[:, 1], signals[:, 0]], axis=1)
        dg_ref[...] = dot_rows(hidden, straight.astype(BF16).reshape(512, DL))
        dh_ref[...] = dot_rows(hidden, swapped.astype(BF16).reshape(512, DL))

    def prefetch():
        loads[7].wait()
        loads[8].wait()
        scaled(dw, ds, wide.at[:, pl.ds(0, DL)], HL, DL)
        loads[9].wait()
        theirs = tok.at[pl.ds(pl.multiple_of((1 - core) * 128, 128), 128)]
        return [
            copies.one(wide.at[:, pl.ds(0, DL)], wide.at[:, pl.ds(DL, DL)], sibling),
            copies.one(wide.at[:, pl.ds(2 * DL, DL)], wide.at[:, pl.ds(3 * DL, DL)], sibling),
            copies.one(theirs, tok_sib, sibling),
        ]

    loads[1].wait()
    loads[2].wait()
    pre(0)
    pl.semaphore_wait(barrier, len(partners))
    send_pre(0)
    loads[3].wait()
    loads[4].wait()
    scaled(gw, gs, gw, DL, HL)
    early = [start_first(q, 0) for q in range(CHUNKS)]
    loads[5].wait()
    loads[6].wait()
    scaled(uw, us, uw, DL, HL)
    pre(1)
    send_pre(1)
    shared = []
    prefetched = []

    def first_steps(q):
        groups = early[q], start_first(q, 1)
        if q == 0:
            prefetched.extend(prefetch())
        return groups

    def second_steps(q, arrivals):
        return [middle_first(q, p, arrivals[p]) for p in range(2)]

    def do_output(q, arrivals):
        if q == 0:
            copies.arrive(*prefetched)
        entries, kept = output(q, arrivals)
        shared.append(kept)
        if q == 1:
            background(BACKGROUND[0])
            turned[...] = tok[...].astype(F32).T.astype(BF16)
        return entries

    def do_middle(q, arrivals):
        entries = middle(q, arrivals)
        if q == 1:
            background(BACKGROUND[1])
        return entries

    def do_cotangent(q, arrivals):
        entries = cotangent(q, arrivals)
        if q == 1:
            background(BACKGROUND[2])
        return entries

    def do_backward(q, arrivals):
        entries, kept = backward(q, arrivals)
        shared.append(kept)
        if q == 1:
            shared.extend(share_multipliers(n) for n in range(CHUNKS))
        return entries

    steps = [first_steps, second_steps, activate, do_output, do_middle, do_cotangent, spread, do_backward, gradients]
    flying = [steps[0](q) for q in range(CHUNKS)]
    for step in steps[1:]:
        flying = [step(q, flying[q]) for q in range(CHUNKS)]

    copies.arrive(*shared)
    for q in range(CHUNKS):
        combine(core, q, place)
    down_products()
    copies.sent()
    passed = []
    for q in range(CHUNKS):
        for near in (1, 0):
            origins = [places_from[k] for k in parts[near]]
            copies.arrive(flying[q][near])
            passed.append((q, origins + [place] * near, pass_on(q, origins + [place] * near)))
            for n in origins:
                combine(core, q, n)
    for q, origins, group in passed:
        copies.arrive(group)
        for n in origins:
            combine(1 - core, q, n)
    copies.sent()
    assert len(copies.groups) == GROUPS_SENT


def exchange(*operands):
    vmem = pl.BlockSpec(memory_space=pltpu.VMEM)
    hbm = pl.BlockSpec(memory_space=pltpu.HBM)
    return pl.pallas_call(
        exchange_kernel,
        out_shape=(
            pltpu.VMEM((2, CHUNKS, GROUPS, 32, HL), BF16),
            pltpu.VMEM((HL, DL), F32),
            pltpu.VMEM((HL, DL), F32),
            pltpu.VMEM((DL, 256), BF16),
        ),
        in_specs=[hbm] * 10,
        out_specs=(vmem, vmem, vmem, vmem),
        scratch_shapes=[
            pltpu.VMEM((256, DL), BF16),
            pltpu.VMEM((128, DL), BF16),
            pltpu.VMEM((256, DL), BF16),
            pltpu.VMEM((2, DL, 2 * HL), BF16),
            pltpu.VMEM((HL, DL), BF16),
            pltpu.VMEM((HL, 4 * DL), BF16),
            pltpu.VMEM((DL,), F32),
            pltpu.VMEM((DL,), F32),
            pltpu.VMEM((HL,), F32),
            pltpu.VMEM((CHUNKS, 2, GROUPS, 16, HL), BF16),
            pltpu.VMEM((CHUNKS, 2, GROUPS, 16, HL), BF16),
            pltpu.VMEM((4, 128, HL), F32),
            pltpu.VMEM((CHUNKS, 2, 4, 2, 16, HL), BF16),
            pltpu.VMEM((CHUNKS, 2, 3, 2, 16, HL), BF16),
            pltpu.VMEM((CHUNKS, 2, 4, 16, HL), BF16),
            pltpu.VMEM((CHUNKS, 2, 4, 16, HL), BF16),
            pltpu.VMEM((CHUNKS, 2, 16, HL), F32),
            pltpu.VMEM((2, CHUNKS, GROUPS, 16, HL), BF16),
            pltpu.VMEM((2, CHUNKS, 2, 4, 16, DL), BF16),
            pltpu.VMEM((2, CHUNKS, GROUPS, 16, HL), BF16),
            pltpu.VMEM((2, CHUNKS, GROUPS, 32, HL), BF16),
            pltpu.VMEM((CHUNKS, 2, 2, 4, 16, DL), BF16),
            pltpu.VMEM((CHUNKS, 3, 4, 16, DL), BF16),
            pltpu.VMEM((CHUNKS, 4, 16, DL), BF16),
            pltpu.VMEM((CHUNKS, 3, 16, DL), BF16),
            pltpu.VMEM((CHUNKS, 2, 2, 4, 16, DL), BF16),
            pltpu.VMEM((CHUNKS, GROUPS, 16, HL), BF16),
            pltpu.VMEM((CHUNKS, len(ZERO_STEPS), 16, HL), BF16),
            pltpu.SemaphoreType.DMA((10,)),
            pltpu.SemaphoreType.DMA((SENDS,)),
            pltpu.SemaphoreType.DMA((GROUPS_SENT,)),
        ],
        compiler_params=pltpu.CompilerParams(
            collective_id=0, has_side_effects=True, vmem_limit_bytes=44 * 2**20
        ),
        name="exchange",
    )(*[pltpu.with_memory_space_constraint(operand, pltpu.HBM) for operand in operands])


def products_kernel(turned, g, down, down_tan, gg, ug, dg, gh, uh, dh, square, sems):
    copies = []

    def put(src, out, first, count):
        rows = pl.ds(first, count)
        copy = pltpu.make_async_copy(src.at[rows], out.at[rows], sems.at[len(copies)])
        copy.start()
        copies.append(copy)

    for src, out in ((down, dg), (down_tan, dh)):
        for half in range(2):
            put(src, out, half * (HL // 2), HL // 2)
    for n, out in enumerate((gg, ug, gh, uh)):
        part = g[:, :, :, (n // 2) * 16 : (n // 2) * 16 + 16, :].astype(F32).reshape(32, 2, ROWS, HL)
        rows = part[:, n % 2].reshape(256, HL).astype(BF16)
        for half in range(2):
            first = half * (DL // 2)
            square[n, first : first + DL // 2] = dot(turned[first : first + DL // 2], rows)
            put(square.at[n], out, first, DL // 2)
    for copy in copies:
        copy.wait()


def products(turned, g, down, down_tan):
    vmem = pl.BlockSpec(memory_space=pltpu.VMEM)
    hbm = pl.BlockSpec(memory_space=pl.ANY)
    tall = jax.ShapeDtypeStruct((DL, HL), F32)
    flat = jax.ShapeDtypeStruct((HL, DL), F32)
    return pl.pallas_call(
        products_kernel,
        out_shape=(tall, tall, flat, tall, tall, flat),
        in_specs=[vmem] * 4,
        out_specs=[hbm] * 6,
        scratch_shapes=[pltpu.VMEM((4, DL, HL), F32), pltpu.SemaphoreType.DMA((12,))],
        compiler_params=pltpu.CompilerParams(vmem_limit_bytes=40 * 2**20),
        name="products",
    )(turned, g, down, down_tan)


def local(
    tokens, gate_weight, up_weight, down_weight, gate_scale, up_scale, down_scale, gate_probe, up_probe, down_probe
):
    g, down, down_tan, turned = exchange(
        tokens, gate_weight, up_weight, down_weight, gate_probe, up_probe, down_probe,
        gate_scale, up_scale, down_scale,
    )
    return products(turned, g, down, down_tan)


def solution(mesh):
    in_specs = (
        P(None, "zero"),
        P("zero", "rep"),
        P("zero", "rep"),
        P("rep", "zero"),
        P("zero"),
        P("zero"),
        P("rep"),
        P("zero", "rep"),
        P("zero", "rep"),
        P("rep", "zero"),
    )
    out_specs = (
        P("zero", "rep"),
        P("zero", "rep"),
        P("rep", "zero"),
        P("zero", "rep"),
        P("zero", "rep"),
        P("rep", "zero"),
    )
    return jax.shard_map(local, mesh=mesh, in_specs=in_specs, out_specs=out_specs, check_vma=False)
```

```python
import functools

import jax
import jax.numpy as jnp
from jax import lax
from jax.experimental import pallas as pl
from jax.experimental.pallas import tpu as pltpu
from jax.sharding import PartitionSpec as P

D = 6144
H = 14336
TOKENS = 256

DL = 384
HL = 896
CHUNKS = 2
GROUPS = 8
ROWS = 8
BACKGROUND = (1, 1)
GROUPS_SENT = 45
SENDS = 12

BF16 = jnp.bfloat16
F32 = jnp.float32
MESH = pl.DeviceIdType.MESH

ZERO_STEPS = ((1, 2), (1, 1), (1, 3), (0, 2), (1, 0), (0, 1), (0, 3))
RING_STEPS = (2, 1, 3)


def dot(left, right):
    return jnp.dot(left, right, preferred_element_type=F32)


def dot_last(left, right):
    return lax.dot_general(left, right, (((1,), (1,)), ((), ())), preferred_element_type=F32)


def dot_rows(left, right):
    return lax.dot_general(left, right, (((0,), (0,)), ((), ())), preferred_element_type=F32)


def pair(first, second):
    width = first.shape[-1]
    return jnp.concatenate([first.reshape(-1, ROWS, width), second.reshape(-1, ROWS, width)], axis=1).astype(BF16)


class Copies:
    def __init__(self, send, recv, device):
        self.send, self.recv, self.device = send, recv, device
        self.groups = []
        self.busy = {}

    def start(self, moves, view):
        n = len(self.groups)
        slot = n % SENDS
        if slot in self.busy:
            self.busy.pop(slot).wait_send()
        for src, dst, device in moves:
            pltpu.make_async_remote_copy(
                src_ref=src, dst_ref=dst, send_sem=self.send.at[slot], recv_sem=self.recv.at[n],
                device_id=device, device_id_type=MESH,
            ).start()
        group = pltpu.make_async_remote_copy(
            src_ref=view, dst_ref=view, send_sem=self.send.at[slot], recv_sem=self.recv.at[n],
            device_id=self.device, device_id_type=MESH,
        )
        self.busy[slot] = group
        self.groups.append(group)
        return group

    def one(self, src, dst, device):
        return self.start([(src, dst, device)], dst)

    def arrive(self, *groups):
        for group in groups:
            group.wait_recv()

    def sent(self):
        for slot in list(self.busy):
            self.busy.pop(slot).wait_send()


def exchange_kernel(
    tok_hbm, gw_hbm, uw_hbm, dw_hbm, gp_hbm, up_hbm, dp_hbm, gs_hbm, us_hbm, ds_hbm,
    g_ref, dg_ref, dh_ref, turned,
    tok, tok_sib, tok_order, mats, dw, wide, gs, us, ds,
    sib_out, sib_in, own, stage, far4, near4, sum4, mine4,
    x_ref, y_ref, hids, mult, outs, outs_in, mids, mids_in, back,
    hid, hid_in,
    load_sem, send_sem, recv_sem, ready,
):
    rep = lax.axis_index("rep")
    zero = lax.axis_index("zero")
    core = lax.rem(zero, 2)
    z_lo, x = lax.div(zero, 8), lax.rem(lax.div(zero, 2), 4)
    z_hi, y = lax.div(rep, 4), lax.rem(rep, 4)
    sibling = (rep, zero + 1 - 2 * core)
    twin = (rep, (1 - z_lo) * 8 + x * 2 + core)
    ring_x = [x] + [lax.rem(x + step, 4) for step in (1, 2, 3)]
    xs = [ring_x[step] for step in RING_STEPS]
    ys = [lax.rem(y + step, 4) for step in RING_STEPS]
    zs = [lax.rem(z_hi + step, 4) for step in RING_STEPS]
    x_peers = [(rep, z_lo * 8 + other * 2 + core) for other in xs]
    y_peers = [(z_hi * 4 + other, zero) for other in ys]
    z_peers = [(other * 4 + y, zero) for other in zs]
    ring_z = [z_lo, 1 - z_lo]
    chips = [(ring_x[dx], ring_z[dz]) for dz, dx in ZERO_STEPS]
    chips_from = [(ring_x[(4 - dx) % 4], ring_z[dz]) for dz, dx in ZERO_STEPS]
    places = [2 * other_x + other_z for other_x, other_z in chips]
    places_from = [2 * other_x + other_z for other_x, other_z in chips_from]
    chip_peers = [(rep, other_z * 8 + other_x * 2 + core) for other_x, other_z in chips]
    partners = [sibling, twin] + x_peers + y_peers + z_peers[1:]
    copies = Copies(send_sem, recv_sem, sibling)

    barrier = pltpu.get_barrier_semaphore()
    for other in partners:
        pl.semaphore_signal(barrier, inc=1, device_id=other, device_id_type=MESH)

    gp, up = mats.at[0, :, pl.ds(0, HL)], mats.at[0, :, pl.ds(HL, HL)]
    gw, uw = mats.at[1, :, pl.ds(0, HL)], mats.at[1, :, pl.ds(HL, HL)]
    pairs = (
        (tok_hbm, tok), (gp_hbm, gp), (up_hbm, up), (gs_hbm, gs), (gw_hbm, gw), (us_hbm, us), (uw_hbm, uw),
        (ds_hbm, ds), (dw_hbm, dw), (dp_hbm, wide.at[:, pl.ds(2 * DL, DL)]),
    )
    loads = [pltpu.make_async_copy(src, dst, load_sem.at[n]) for n, (src, dst) in enumerate(pairs)]
    for copy in loads:
        copy.start()

    loads[0].wait()
    tok_order[0:128, :] = tok[pl.ds(pl.multiple_of((1 - core) * 128, 128), 128), :]
    tok_order[128:256, :] = tok[pl.ds(pl.multiple_of(core * 128, 128), 128), :]
    tokens = tok_order[...]

    def scaled(ref, scale_ref, out_ref, rows, width):
        column = jnp.broadcast_to(scale_ref[...].reshape(1, rows), (128, rows)).T
        for n in range(width // 128):
            block = slice(n * 128, (n + 1) * 128)
            out_ref[:, block] = (ref[:, block].astype(F32) * column).astype(BF16)

    from_sib = {}

    def pre(p):
        wide_result = dot(tokens, mats[p])
        a, b = wide_result[:, 0:HL], wide_result[:, HL : 2 * HL]
        own[2 * p] = a[128:256]
        own[2 * p + 1] = b[128:256]
        both = pair(a[0:128], b[0:128])
        for q in range(CHUNKS):
            sib_out[q, p] = both[q * GROUPS : (q + 1) * GROUPS]

    def send_pre(p):
        for q in range(CHUNKS):
            from_sib[q, p] = copies.one(sib_out.at[q, p], sib_in.at[q, p], sibling)

    def sum_start(q, parts, far, near):
        if q == 0:
            return copies.start([(parts.at[other], far.at[k], x_peers[k]) for k, other in enumerate(xs)], far)
        return copies.one(parts.at[:, 1 - z_lo], near, twin)

    def sum_middle(q, parts, far, near, out, mine, ours, arrival):
        copies.arrive(arrival)
        if q == 0:
            total = ours
            for k in range(3):
                total = total + far[k].astype(F32)
            mine[...] = jnp.where(z_lo == 0, total[0], total[1])
            out[0] = jnp.where(z_lo == 0, total[1], total[0]).astype(BF16)
            return copies.one(out.at[0], near.at[0], twin)
        out[...] = (parts[:, z_lo].astype(F32) + near[...].astype(F32)).astype(BF16)
        group = copies.start(
            [(out.at[other], far.at[k, 0], x_peers[k]) for k, other in enumerate(xs)], far.at[:, 0]
        )
        mine[...] = ours + near[x].astype(F32)
        return group

    def sum_end(q, far, near, mine, arrival):
        copies.arrive(arrival)
        total = mine[...]
        if q == 0:
            return total + near[0].astype(F32)
        for k in range(3):
            total = total + far[k, 0].astype(F32)
        return total

    place = 2 * x + z_lo

    def gather(blocks, steps):
        block = blocks.at[place]
        return copies.start([(block, block, chip_peers[k]) for k in steps], blocks.at[pl.ds(0, len(steps))])

    feature_factor = float(D) ** -0.5
    hidden_factor = float(H) ** -0.5
    factor = float(TOKENS) ** -0.5

    def start_first(q, p):
        copies.arrive(from_sib[q, p])
        a = own[2 * p, q * 64 : (q + 1) * 64].reshape(GROUPS, ROWS, HL)
        b = own[2 * p + 1, q * 64 : (q + 1) * 64].reshape(GROUPS, ROWS, HL)
        both = (jnp.concatenate([a, b], axis=1) + sib_in[q, p].astype(F32)).astype(BF16)
        stage[q, p] = both.reshape(4, 2, 16, HL)
        return sum_start(q, stage.at[q, p], far4.at[q, p], near4.at[q, p])

    def middle_first(q, p, arrivals):
        count = 2 if q == 0 else 1
        group = x * 2 if q == 0 else x * 2 + z_lo
        rows = pl.ds(pl.multiple_of(q * 64 + group * ROWS, ROWS), count * ROWS)
        kept = [own[2 * p + n, rows, :].reshape(count, ROWS, HL) for n in range(2)]
        ours = jnp.concatenate(kept, axis=1) + sib_in[q, p, pl.ds(group, count)].astype(F32)
        if q == 1:
            ours = ours[0]
        return sum_middle(
            q, stage.at[q, p], far4.at[q, p], near4.at[q, p], sum4.at[q, p], mine4.at[q, p], ours, arrivals
        )

    multipliers = []

    def activate(q, arrivals):
        totals = [
            sum_end(q, far4.at[q, p], near4.at[q, p], mine4.at[q, p], arrivals[p]) for p in range(2)
        ]
        gate_tan, up_tan, gate_pre, up_pre = [total[n : n + ROWS] for total in totals for n in (0, ROWS)]
        gate_tan = feature_factor * gate_tan
        up_tan = feature_factor * up_tan
        logistic = jax.nn.sigmoid(gate_pre)
        act = gate_pre * logistic
        slope = logistic * (1.0 + gate_pre * (1.0 - logistic))
        bend = logistic * (1.0 - logistic) * (2.0 + gate_pre * (1.0 - 2.0 * logistic))
        lean = slope * gate_tan
        x_ref[core, q, place] = jnp.concatenate([act * up_pre, lean * up_pre + act * up_tan], axis=0).astype(BF16)
        group = gather(x_ref.at[core, q], range(len(chips)))
        mult[core, q, place] = jnp.concatenate(
            [up_pre * slope, act, up_tan * slope + up_pre * bend * gate_tan, lean], axis=0
        ).astype(BF16)
        return group

    def start_multipliers(q):
        block = mult.at[core, q, place]
        multipliers.append(copies.one(block, block, twin))

    waiting = list(range(CHUNKS))

    def background(count):
        for q in waiting[:count]:
            copies.arrive(multipliers[q])
            block = mult.at[core, q, pl.ds(2 * x, 2)]
            multipliers[q] = copies.start([(block, block, peer) for peer in x_peers], mult.at[core, q, pl.ds(0, 6)])
        del waiting[:count]

    def share_multipliers(q):
        copies.arrive(multipliers[q])
        return copies.one(mult.at[core, q], mult.at[core, q], sibling)

    def output(q, arrival):
        copies.arrive(arrival)
        hidden = x_ref[core, q].reshape(GROUPS * 16, HL)
        result = dot(hidden, wide[...])
        for f in range(2):
            straight = result[:, f * DL : (f + 1) * DL].reshape(GROUPS, 2, ROWS, DL)
            probed = result[:, (f + 2) * DL : (f + 3) * DL].reshape(GROUPS, 2, ROWS, DL)
            outs[q, f] = jnp.concatenate(
                [straight[:, 0], hidden_factor * probed[:, 0] + straight[:, 1]], axis=1
            ).astype(BF16).reshape(2, 4, 16, DL)
        group = copies.start(
            [(outs.at[q, lax.rem(other, 2), lax.div(other, 2)], outs_in.at[q, k], y_peers[k]) for k, other in enumerate(ys)],
            outs_in.at[q],
        )
        return group

    half, high = lax.rem(y, 2), lax.div(y, 2)

    def middle(q, arrival):
        copies.arrive(arrival)
        total = outs[q, half, high].astype(F32)
        for k in range(3):
            total += outs_in[q, k].astype(F32)
        mids[q] = total.astype(BF16)
        return copies.start(
            [(mids.at[q, other], mids_in.at[q, k], z_peers[k]) for k, other in enumerate(zs)], mids_in.at[q]
        )

    def cotangent(q, arrival):
        copies.arrive(arrival)
        total = mids[q, z_hi].astype(F32)
        for k in range(3):
            total += mids_in[q, k].astype(F32)
        row = pl.multiple_of(q * 64 + high * 32 + lax.div(z_hi, 2) * 16, 16)
        own_tokens = tok[pl.ds(pl.multiple_of(core * 128 + row, 16), 16), :].astype(F32)
        sib_tokens = tok_sib[pl.ds(row, 16), :].astype(F32)
        chosen = jnp.where(half == 0, own_tokens, sib_tokens)
        chosen = jnp.where(lax.rem(z_hi, 2) == 0, chosen[0:8], chosen[8:16])
        back[q, half, high, z_hi] = jnp.concatenate(
            [factor * (chosen + total[0:8]), factor * total[8:16]], axis=0
        ).astype(BF16)
        block = back.at[q, half, high, z_hi]
        return copies.start([(block, block, peer) for peer in z_peers], back.at[q, half, high, pl.ds(0, 3)])

    def spread(q, arrival):
        copies.arrive(arrival)
        block = back.at[q, half, high]
        return copies.start([(block, block, peer) for peer in y_peers], outs_in.at[q])

    def backward(q, arrival):
        copies.arrive(arrival)
        signals = jnp.concatenate([back[q, f].reshape(GROUPS * 16, DL) for f in range(2)], axis=1)
        straight = dot_last(signals, wide[:, 0 : 2 * DL]).reshape(GROUPS, 2, ROWS, HL)
        probed = dot_last(signals, wide[:, 2 * DL : 4 * DL]).reshape(GROUPS, 2, ROWS, HL)
        both = jnp.concatenate([straight[:, 0], straight[:, 1] + hidden_factor * probed[:, 0]], axis=1)
        hid[q] = both.astype(BF16)
        group = copies.start(
            [(hid.at[q, other], hid_in.at[q, k], chip_peers[k]) for k, other in enumerate(places)], hid_in.at[q]
        )
        return group

    def share_signals(q):
        y_ref[core, q] = back[q, 0]
        return copies.one(back.at[q, 1], y_ref.at[core, q], sibling)

    parts = (range(0, 4), range(4, 7))

    def pass_on(q, origins):
        blocks = [hids.at[core, q, n] for n in origins]
        return copies.start([(block, block, sibling) for block in blocks], hids.at[core, q, pl.ds(0, len(blocks))])

    def gradients(q, arrival):
        copies.arrive(arrival)
        total = hid[q, place].astype(F32)
        for k in range(len(chips)):
            total += hid_in[q, k].astype(F32)
        hids[core, q, place] = total.astype(BF16)
        return [gather(hids.at[core, q], steps) for steps in parts]

    def combine(side, q, n):
        signals = hids[side, q, n].astype(F32)
        signal, signal_tan = signals[0:8], signals[8:16]
        factors = mult[side, q, n].astype(F32)
        first, second, third, fourth = [factors[m * ROWS : (m + 1) * ROWS] for m in range(4)]
        g_ref[side, q, n] = jnp.concatenate(
            [
                signal * first,
                signal * second,
                signal_tan * first + signal * third,
                signal_tan * second + signal * fourth,
            ],
            axis=0,
        ).astype(BF16)

    def down_products():
        hidden = x_ref[...].reshape(512, HL)
        signals = y_ref[...].astype(F32).reshape(32, 2, ROWS, DL)
        straight = jnp.concatenate([signals[:, 0], jnp.zeros_like(signals[:, 0])], axis=1)
        swapped = jnp.concatenate([signals[:, 1], signals[:, 0]], axis=1)
        dg_ref[...] = dot_rows(hidden, straight.astype(BF16).reshape(512, DL))
        dh_ref[...] = dot_rows(hidden, swapped.astype(BF16).reshape(512, DL))

    def prefetch():
        loads[7].wait()
        loads[8].wait()
        scaled(dw, ds, wide.at[:, pl.ds(0, DL)], HL, DL)
        loads[9].wait()
        theirs = tok.at[pl.ds(pl.multiple_of((1 - core) * 128, 128), 128)]
        return [
            copies.one(wide.at[:, pl.ds(0, DL)], wide.at[:, pl.ds(DL, DL)], sibling),
            copies.one(wide.at[:, pl.ds(2 * DL, DL)], wide.at[:, pl.ds(3 * DL, DL)], sibling),
            copies.one(theirs, tok_sib, sibling),
        ]

    loads[1].wait()
    loads[2].wait()
    pre(0)
    pl.semaphore_wait(barrier, len(partners))
    for other in z_peers[1:]:
        pl.semaphore_signal(ready, inc=1, device_id=other, device_id_type=MESH)
    send_pre(0)
    loads[3].wait()
    loads[4].wait()
    scaled(gw, gs, gw, DL, HL)
    early = [start_first(q, 0) for q in range(CHUNKS)]
    loads[5].wait()
    loads[6].wait()
    scaled(uw, us, uw, DL, HL)
    pre(1)
    send_pre(1)
    shared = []
    prefetched = []

    def first_steps(q):
        groups = early[q], start_first(q, 1)
        if q == 1:
            prefetched.extend(prefetch())
        return groups

    def second_steps(q, arrivals):
        return [middle_first(q, p, arrivals[p]) for p in range(2)]

    def do_output(q, arrivals):
        if q == 0:
            copies.arrive(*prefetched)
        entries = output(q, arrivals)
        if q == 1:
            for n in range(CHUNKS):
                start_multipliers(n)
            shared.extend(copies.one(x_ref.at[core, n], x_ref.at[core, n], sibling) for n in range(CHUNKS))
            turned[...] = tok[...].astype(F32).T.astype(BF16)
        return entries

    def do_middle(q, arrivals):
        if q == 0:
            pl.semaphore_wait(ready, 2)
        entries = middle(q, arrivals)
        if q == 1:
            background(BACKGROUND[0])
        return entries

    def do_cotangent(q, arrivals):
        entries = cotangent(q, arrivals)
        if q == 1:
            background(BACKGROUND[1])
        return entries

    def do_spread(q, arrivals):
        group = spread(q, arrivals)
        if q == 1:
            shared.append(share_multipliers(0))
        return group

    def do_backward(q, arrivals):
        entries = backward(q, arrivals)
        if q == 1:
            shared.extend(share_signals(n) for n in range(CHUNKS))
            shared.append(share_multipliers(1))
        return entries

    steps = [first_steps, second_steps, activate, do_output, do_middle, do_cotangent, do_spread, do_backward, gradients]
    flying = [steps[0](q) for q in range(CHUNKS)]
    for step in steps[1:]:
        flying = [step(q, flying[q]) for q in range(CHUNKS)]

    copies.arrive(*shared)
    for q in range(CHUNKS):
        combine(core, q, place)
    down_products()
    copies.sent()
    passed = []
    for q in range(CHUNKS):
        for near in (1, 0):
            origins = [places_from[k] for k in parts[near]]
            copies.arrive(flying[q][near])
            passed.append((q, origins + [place] * near, pass_on(q, origins + [place] * near)))
            for n in origins:
                combine(core, q, n)
    for q, origins, group in passed:
        copies.arrive(group)
        for n in origins:
            combine(1 - core, q, n)
    copies.sent()
    assert len(copies.groups) == GROUPS_SENT


def exchange(*operands):
    vmem = pl.BlockSpec(memory_space=pltpu.VMEM)
    hbm = pl.BlockSpec(memory_space=pltpu.HBM)
    return pl.pallas_call(
        exchange_kernel,
        out_shape=(
            pltpu.VMEM((2, CHUNKS, GROUPS, 32, HL), BF16),
            pltpu.VMEM((HL, DL), F32),
            pltpu.VMEM((HL, DL), F32),
            pltpu.VMEM((DL, 256), BF16),
        ),
        in_specs=[hbm] * 10,
        out_specs=(vmem, vmem, vmem, vmem),
        scratch_shapes=[
            pltpu.VMEM((256, DL), BF16),
            pltpu.VMEM((128, DL), BF16),
            pltpu.VMEM((256, DL), BF16),
            pltpu.VMEM((2, DL, 2 * HL), BF16),
            pltpu.VMEM((HL, DL), BF16),
            pltpu.VMEM((HL, 4 * DL), BF16),
            pltpu.VMEM((DL,), F32),
            pltpu.VMEM((DL,), F32),
            pltpu.VMEM((HL,), F32),
            pltpu.VMEM((CHUNKS, 2, GROUPS, 16, HL), BF16),
            pltpu.VMEM((CHUNKS, 2, GROUPS, 16, HL), BF16),
            pltpu.VMEM((4, 128, HL), F32),
            pltpu.VMEM((CHUNKS, 2, 4, 2, 16, HL), BF16),
            pltpu.VMEM((CHUNKS, 2, 3, 2, 16, HL), BF16),
            pltpu.VMEM((CHUNKS, 2, 4, 16, HL), BF16),
            pltpu.VMEM((CHUNKS, 2, 4, 16, HL), BF16),
            pltpu.VMEM((CHUNKS, 2, 16, HL), F32),
            pltpu.VMEM((2, CHUNKS, GROUPS, 16, HL), BF16),
            pltpu.VMEM((2, CHUNKS, 2, 4, 16, DL), BF16),
            pltpu.VMEM((2, CHUNKS, GROUPS, 16, HL), BF16),
            pltpu.VMEM((2, CHUNKS, GROUPS, 32, HL), BF16),
            pltpu.VMEM((CHUNKS, 2, 2, 4, 16, DL), BF16),
            pltpu.VMEM((CHUNKS, 3, 4, 16, DL), BF16),
            pltpu.VMEM((CHUNKS, 4, 16, DL), BF16),
            pltpu.VMEM((CHUNKS, 3, 16, DL), BF16),
            pltpu.VMEM((CHUNKS, 2, 2, 4, 16, DL), BF16),
            pltpu.VMEM((CHUNKS, GROUPS, 16, HL), BF16),
            pltpu.VMEM((CHUNKS, len(ZERO_STEPS), 16, HL), BF16),
            pltpu.SemaphoreType.DMA((10,)),
            pltpu.SemaphoreType.DMA((SENDS,)),
            pltpu.SemaphoreType.DMA((GROUPS_SENT,)),
            pltpu.SemaphoreType.REGULAR,
        ],
        compiler_params=pltpu.CompilerParams(
            collective_id=0, has_side_effects=True, vmem_limit_bytes=44 * 2**20
        ),
        name="exchange",
    )(*[pltpu.with_memory_space_constraint(operand, pltpu.HBM) for operand in operands])


def products_kernel(turned, g, down, down_tan, gg, ug, dg, gh, uh, dh, square, sems):
    copies = []

    def put(src, out, first, count):
        rows = pl.ds(first, count)
        copy = pltpu.make_async_copy(src.at[rows], out.at[rows], sems.at[len(copies)])
        copy.start()
        copies.append(copy)

    for src, out in ((down, dg), (down_tan, dh)):
        for half in range(2):
            put(src, out, half * (HL // 2), HL // 2)
    for n, out in enumerate((gg, ug, gh, uh)):
        part = g[:, :, :, (n // 2) * 16 : (n // 2) * 16 + 16, :].astype(F32).reshape(32, 2, ROWS, HL)
        rows = part[:, n % 2].reshape(256, HL).astype(BF16)
        for half in range(2):
            first = half * (DL // 2)
            square[n, first : first + DL // 2] = dot(turned[first : first + DL // 2], rows)
            put(square.at[n], out, first, DL // 2)
    for copy in copies:
        copy.wait()


def products(turned, g, down, down_tan):
    vmem = pl.BlockSpec(memory_space=pltpu.VMEM)
    hbm = pl.BlockSpec(memory_space=pl.ANY)
    tall = jax.ShapeDtypeStruct((DL, HL), F32)
    flat = jax.ShapeDtypeStruct((HL, DL), F32)
    return pl.pallas_call(
        products_kernel,
        out_shape=(tall, tall, flat, tall, tall, flat),
        in_specs=[vmem] * 4,
        out_specs=[hbm] * 6,
        scratch_shapes=[pltpu.VMEM((4, DL, HL), F32), pltpu.SemaphoreType.DMA((12,))],
        compiler_params=pltpu.CompilerParams(vmem_limit_bytes=40 * 2**20),
        name="products",
    )(turned, g, down, down_tan)


def local(
    tokens, gate_weight, up_weight, down_weight, gate_scale, up_scale, down_scale, gate_probe, up_probe, down_probe
):
    g, down, down_tan, turned = exchange(
        tokens, gate_weight, up_weight, down_weight, gate_probe, up_probe, down_probe,
        gate_scale, up_scale, down_scale,
    )
    return products(turned, g, down, down_tan)


def solution(mesh):
    in_specs = (
        P(None, "zero"),
        P("zero", "rep"),
        P("zero", "rep"),
        P("rep", "zero"),
        P("zero"),
        P("zero"),
        P("rep"),
        P("zero", "rep"),
        P("zero", "rep"),
        P("rep", "zero"),
    )
    out_specs = (
        P("zero", "rep"),
        P("zero", "rep"),
        P("rep", "zero"),
        P("zero", "rep"),
        P("zero", "rep"),
        P("rep", "zero"),
    )
    return jax.shard_map(local, mesh=mesh, in_specs=in_specs, out_specs=out_specs, check_vma=False)
```

```python
import functools

import jax
import jax.numpy as jnp
from jax import lax
from jax.experimental import pallas as pl
from jax.experimental.pallas import tpu as pltpu
from jax.sharding import PartitionSpec as P

D = 6144
H = 14336
TOKENS = 256

DL = 384
HL = 896
CHUNKS = 2
GROUPS = 8
ROWS = 8
BACKGROUND = (1, 1)
GROUPS_SENT = 45
SENDS = 12

BF16 = jnp.bfloat16
F32 = jnp.float32
MESH = pl.DeviceIdType.MESH

ZERO_STEPS = ((1, 2), (1, 1), (1, 3), (0, 2), (1, 0), (0, 1), (0, 3))
RING_STEPS = (2, 1, 3)


def dot(left, right):
    return jnp.dot(left, right, preferred_element_type=F32)


def dot_last(left, right):
    return lax.dot_general(left, right, (((1,), (1,)), ((), ())), preferred_element_type=F32)


def dot_rows(left, right):
    return lax.dot_general(left, right, (((0,), (0,)), ((), ())), preferred_element_type=F32)


def pair(first, second):
    width = first.shape[-1]
    return jnp.concatenate([first.reshape(-1, ROWS, width), second.reshape(-1, ROWS, width)], axis=1).astype(BF16)


class Copies:
    def __init__(self, send, recv, device):
        self.send, self.recv, self.device = send, recv, device
        self.groups = []
        self.busy = {}

    def start(self, moves, view):
        n = len(self.groups)
        slot = n % SENDS
        if slot in self.busy:
            self.busy.pop(slot).wait_send()
        for src, dst, device in moves:
            pltpu.make_async_remote_copy(
                src_ref=src, dst_ref=dst, send_sem=self.send.at[slot], recv_sem=self.recv.at[n],
                device_id=device, device_id_type=MESH,
            ).start()
        group = pltpu.make_async_remote_copy(
            src_ref=view, dst_ref=view, send_sem=self.send.at[slot], recv_sem=self.recv.at[n],
            device_id=self.device, device_id_type=MESH,
        )
        self.busy[slot] = group
        self.groups.append(group)
        return group

    def one(self, src, dst, device):
        return self.start([(src, dst, device)], dst)

    def arrive(self, *groups):
        for group in groups:
            group.wait_recv()

    def sent(self):
        for slot in list(self.busy):
            self.busy.pop(slot).wait_send()


def exchange_kernel(
    tok_hbm, gw_hbm, uw_hbm, dw_hbm, gp_hbm, up_hbm, dp_hbm, gs_hbm, us_hbm, ds_hbm,
    g_ref, dg_ref, dh_ref, turned,
    tok, tok_sib, tok_order, mats, dw, wide, gs, us, ds,
    sib_out, sib_in, own, stage, far4, near4, sum4, mine4,
    x_ref, y_ref, hids, mult, outs, outs_in, mids, mids_in, back,
    hid, hid_in,
    load_sem, send_sem, recv_sem, ready,
):
    rep = lax.axis_index("rep")
    zero = lax.axis_index("zero")
    core = lax.rem(zero, 2)
    z_lo, x = lax.div(zero, 8), lax.rem(lax.div(zero, 2), 4)
    z_hi, y = lax.div(rep, 4), lax.rem(rep, 4)
    sibling = (rep, zero + 1 - 2 * core)
    twin = (rep, (1 - z_lo) * 8 + x * 2 + core)
    ring_x = [x] + [lax.rem(x + step, 4) for step in (1, 2, 3)]
    xs = [ring_x[step] for step in RING_STEPS]
    ys = [lax.rem(y + step, 4) for step in RING_STEPS]
    zs = [lax.rem(z_hi + step, 4) for step in RING_STEPS]
    x_peers = [(rep, z_lo * 8 + other * 2 + core) for other in xs]
    y_peers = [(z_hi * 4 + other, zero) for other in ys]
    z_peers = [(other * 4 + y, zero) for other in zs]
    ring_z = [z_lo, 1 - z_lo]
    chips = [(ring_x[dx], ring_z[dz]) for dz, dx in ZERO_STEPS]
    chips_from = [(ring_x[(4 - dx) % 4], ring_z[dz]) for dz, dx in ZERO_STEPS]
    places = [2 * other_x + other_z for other_x, other_z in chips]
    places_from = [2 * other_x + other_z for other_x, other_z in chips_from]
    chip_peers = [(rep, other_z * 8 + other_x * 2 + core) for other_x, other_z in chips]
    partners = [sibling, twin] + x_peers + y_peers + z_peers[1:]
    copies = Copies(send_sem, recv_sem, sibling)

    barrier = pltpu.get_barrier_semaphore()
    for other in partners:
        pl.semaphore_signal(barrier, inc=1, device_id=other, device_id_type=MESH)

    gp, up = mats.at[0, :, pl.ds(0, HL)], mats.at[0, :, pl.ds(HL, HL)]
    gw, uw = mats.at[1, :, pl.ds(0, HL)], mats.at[1, :, pl.ds(HL, HL)]
    pairs = (
        (tok_hbm, tok), (gp_hbm, gp), (up_hbm, up), (gs_hbm, gs), (gw_hbm, gw), (us_hbm, us), (uw_hbm, uw),
        (ds_hbm, ds), (dw_hbm, dw), (dp_hbm, wide.at[:, pl.ds(2 * DL, DL)]),
    )
    loads = [pltpu.make_async_copy(src, dst, load_sem.at[n]) for n, (src, dst) in enumerate(pairs)]
    for copy in loads:
        copy.start()

    loads[0].wait()
    tok_order[0:128, :] = tok[pl.ds(pl.multiple_of((1 - core) * 128, 128), 128), :]
    tok_order[128:256, :] = tok[pl.ds(pl.multiple_of(core * 128, 128), 128), :]
    tokens = tok_order[...]

    def scaled(ref, scale_ref, out_ref, rows, width):
        column = jnp.broadcast_to(scale_ref[...].reshape(1, rows), (128, rows)).T
        for n in range(width // 128):
            block = slice(n * 128, (n + 1) * 128)
            out_ref[:, block] = (ref[:, block].astype(F32) * column).astype(BF16)

    from_sib = {}

    def pre(p):
        wide_result = dot(tokens, mats[p])
        a, b = wide_result[:, 0:HL], wide_result[:, HL : 2 * HL]
        own[2 * p] = a[128:256]
        own[2 * p + 1] = b[128:256]
        both = pair(a[0:128], b[0:128])
        for q in range(CHUNKS):
            sib_out[q, p] = both[q * GROUPS : (q + 1) * GROUPS]

    def send_pre(p):
        for q in range(CHUNKS):
            from_sib[q, p] = copies.one(sib_out.at[q, p], sib_in.at[q, p], sibling)

    def sum_start(q, parts, far, near):
        if q == 0:
            return copies.start([(parts.at[other], far.at[k], x_peers[k]) for k, other in enumerate(xs)], far)
        return copies.one(parts.at[:, 1 - z_lo], near, twin)

    def sum_middle(q, parts, far, near, out, mine, ours, arrival):
        copies.arrive(arrival)
        if q == 0:
            total = ours
            for k in range(3):
                total = total + far[k].astype(F32)
            mine[...] = jnp.where(z_lo == 0, total[0], total[1])
            out[0] = jnp.where(z_lo == 0, total[1], total[0]).astype(BF16)
            return copies.one(out.at[0], near.at[0], twin)
        out[...] = (parts[:, z_lo].astype(F32) + near[...].astype(F32)).astype(BF16)
        group = copies.start(
            [(out.at[other], far.at[k, 0], x_peers[k]) for k, other in enumerate(xs)], far.at[:, 0]
        )
        mine[...] = ours + near[x].astype(F32)
        return group

    def sum_end(q, far, near, mine, arrival):
        copies.arrive(arrival)
        total = mine[...]
        if q == 0:
            return total + near[0].astype(F32)
        for k in range(3):
            total = total + far[k, 0].astype(F32)
        return total

    place = 2 * x + z_lo

    def gather(blocks, steps):
        block = blocks.at[place]
        return copies.start([(block, block, chip_peers[k]) for k in steps], blocks.at[pl.ds(0, len(steps))])

    feature_factor = float(D) ** -0.5
    hidden_factor = float(H) ** -0.5
    factor = float(TOKENS) ** -0.5

    def start_first(q, p):
        copies.arrive(from_sib[q, p])
        a = own[2 * p, q * 64 : (q + 1) * 64].reshape(GROUPS, ROWS, HL)
        b = own[2 * p + 1, q * 64 : (q + 1) * 64].reshape(GROUPS, ROWS, HL)
        both = (jnp.concatenate([a, b], axis=1) + sib_in[q, p].astype(F32)).astype(BF16)
        stage[q, p] = both.reshape(4, 2, 16, HL)
        return sum_start(q, stage.at[q, p], far4.at[q, p], near4.at[q, p])

    def middle_first(q, p, arrivals):
        count = 2 if q == 0 else 1
        group = x * 2 if q == 0 else x * 2 + z_lo
        rows = pl.ds(pl.multiple_of(q * 64 + group * ROWS, ROWS), count * ROWS)
        kept = [own[2 * p + n, rows, :].reshape(count, ROWS, HL) for n in range(2)]
        ours = jnp.concatenate(kept, axis=1) + sib_in[q, p, pl.ds(group, count)].astype(F32)
        if q == 1:
            ours = ours[0]
        return sum_middle(
            q, stage.at[q, p], far4.at[q, p], near4.at[q, p], sum4.at[q, p], mine4.at[q, p], ours, arrivals
        )

    multipliers = []

    def activate(q, arrivals):
        totals = [
            sum_end(q, far4.at[q, p], near4.at[q, p], mine4.at[q, p], arrivals[p]) for p in range(2)
        ]
        gate_tan, up_tan, gate_pre, up_pre = [total[n : n + ROWS] for total in totals for n in (0, ROWS)]
        gate_tan = feature_factor * gate_tan
        up_tan = feature_factor * up_tan
        logistic = jax.nn.sigmoid(gate_pre)
        act = gate_pre * logistic
        slope = logistic * (1.0 + gate_pre * (1.0 - logistic))
        bend = logistic * (1.0 - logistic) * (2.0 + gate_pre * (1.0 - 2.0 * logistic))
        lean = slope * gate_tan
        x_ref[core, q, place] = jnp.concatenate([act * up_pre, lean * up_pre + act * up_tan], axis=0).astype(BF16)
        group = gather(x_ref.at[core, q], range(len(chips)))
        mult[core, q, place] = jnp.concatenate(
            [up_pre * slope, act, up_tan * slope + up_pre * bend * gate_tan, lean], axis=0
        ).astype(BF16)
        return group

    def start_multipliers(q):
        block = mult.at[core, q, place]
        multipliers.append(copies.one(block, block, twin))

    waiting = list(range(CHUNKS))

    def background(count):
        for q in waiting[:count]:
            copies.arrive(multipliers[q])
            block = mult.at[core, q, pl.ds(2 * x, 2)]
            multipliers[q] = copies.start([(block, block, peer) for peer in x_peers], mult.at[core, q, pl.ds(0, 6)])
        del waiting[:count]

    def share_multipliers(q):
        copies.arrive(multipliers[q])
        return copies.one(mult.at[core, q], mult.at[core, q], sibling)

    def output(q, arrival):
        copies.arrive(arrival)
        hidden = x_ref[core, q].reshape(GROUPS * 16, HL)
        result = dot(hidden, wide[...])
        for f in range(2):
            straight = result[:, f * DL : (f + 1) * DL].reshape(GROUPS, 2, ROWS, DL)
            probed = result[:, (f + 2) * DL : (f + 3) * DL].reshape(GROUPS, 2, ROWS, DL)
            outs[q, f] = jnp.concatenate(
                [straight[:, 0], hidden_factor * probed[:, 0] + straight[:, 1]], axis=1
            ).astype(BF16).reshape(2, 4, 16, DL)
        group = copies.start(
            [(outs.at[q, lax.rem(other, 2), lax.div(other, 2)], outs_in.at[q, k], y_peers[k]) for k, other in enumerate(ys)],
            outs_in.at[q],
        )
        return group

    half, high = lax.rem(y, 2), lax.div(y, 2)

    def middle(q, arrival):
        copies.arrive(arrival)
        total = outs[q, half, high].astype(F32)
        for k in range(3):
            total += outs_in[q, k].astype(F32)
        mids[q] = total.astype(BF16)
        return copies.start(
            [(mids.at[q, other], mids_in.at[q, k], z_peers[k]) for k, other in enumerate(zs)], mids_in.at[q]
        )

    def cotangent(q, arrival):
        copies.arrive(arrival)
        total = mids[q, z_hi].astype(F32)
        for k in range(3):
            total += mids_in[q, k].astype(F32)
        row = pl.multiple_of(q * 64 + high * 32 + lax.div(z_hi, 2) * 16, 16)
        own_tokens = tok[pl.ds(pl.multiple_of(core * 128 + row, 16), 16), :].astype(F32)
        sib_tokens = tok_sib[pl.ds(row, 16), :].astype(F32)
        chosen = jnp.where(half == 0, own_tokens, sib_tokens)
        chosen = jnp.where(lax.rem(z_hi, 2) == 0, chosen[0:8], chosen[8:16])
        back[q, half, high, z_hi] = jnp.concatenate(
            [factor * (chosen + total[0:8]), factor * total[8:16]], axis=0
        ).astype(BF16)
        block = back.at[q, half, high, z_hi]
        return copies.start([(block, block, peer) for peer in z_peers], back.at[q, half, high, pl.ds(0, 3)])

    def spread(q, arrival):
        copies.arrive(arrival)
        block = back.at[q, half, high]
        return copies.start([(block, block, peer) for peer in y_peers], outs_in.at[q])

    def backward(q, arrival):
        copies.arrive(arrival)
        signals = jnp.concatenate([back[q, f].reshape(GROUPS * 16, DL) for f in range(2)], axis=1)
        straight = dot_last(signals, wide[:, 0 : 2 * DL]).reshape(GROUPS, 2, ROWS, HL)
        probed = dot_last(signals, wide[:, 2 * DL : 4 * DL]).reshape(GROUPS, 2, ROWS, HL)
        both = jnp.concatenate([straight[:, 0], straight[:, 1] + hidden_factor * probed[:, 0]], axis=1)
        hid[q] = both.astype(BF16)
        group = copies.start(
            [(hid.at[q, other], hid_in.at[q, k], chip_peers[k]) for k, other in enumerate(places)], hid_in.at[q]
        )
        return group

    def share_signals(q):
        y_ref[core, q] = back[q, 0]
        return copies.one(back.at[q, 1], y_ref.at[core, q], sibling)

    parts = (range(0, 4), range(4, 7))

    def pass_on(q, origins):
        blocks = [hids.at[core, q, n] for n in origins]
        return copies.start([(block, block, sibling) for block in blocks], hids.at[core, q, pl.ds(0, len(blocks))])

    def gradients(q, arrival):
        copies.arrive(arrival)
        total = hid[q, place].astype(F32)
        for k in range(len(chips)):
            total += hid_in[q, k].astype(F32)
        hids[core, q, place] = total.astype(BF16)
        return [gather(hids.at[core, q], steps) for steps in parts]

    def combine(side, q, n):
        signals = hids[side, q, n].astype(F32)
        signal, signal_tan = signals[0:8], signals[8:16]
        factors = mult[side, q, n].astype(F32)
        first, second, third, fourth = [factors[m * ROWS : (m + 1) * ROWS] for m in range(4)]
        g_ref[side, q, n] = jnp.concatenate(
            [
                signal * first,
                signal * second,
                signal_tan * first + signal * third,
                signal_tan * second + signal * fourth,
            ],
            axis=0,
        ).astype(BF16)

    def down_products():
        hidden = x_ref[...].reshape(512, HL)
        signals = y_ref[...].astype(F32).reshape(32, 2, ROWS, DL)
        straight = jnp.concatenate([signals[:, 0], jnp.zeros_like(signals[:, 0])], axis=1)
        swapped = jnp.concatenate([signals[:, 1], signals[:, 0]], axis=1)
        dg_ref[...] = dot_rows(hidden, straight.astype(BF16).reshape(512, DL))
        dh_ref[...] = dot_rows(hidden, swapped.astype(BF16).reshape(512, DL))

    def prefetch():
        loads[7].wait()
        loads[8].wait()
        scaled(dw, ds, wide.at[:, pl.ds(0, DL)], HL, DL)
        loads[9].wait()
        theirs = tok.at[pl.ds(pl.multiple_of((1 - core) * 128, 128), 128)]
        return [
            copies.one(wide.at[:, pl.ds(0, DL)], wide.at[:, pl.ds(DL, DL)], sibling),
            copies.one(wide.at[:, pl.ds(2 * DL, DL)], wide.at[:, pl.ds(3 * DL, DL)], sibling),
            copies.one(theirs, tok_sib, sibling),
        ]

    loads[1].wait()
    loads[2].wait()
    pre(0)
    pl.semaphore_wait(barrier, len(partners))
    for other in z_peers[1:]:
        pl.semaphore_signal(ready, inc=1, device_id=other, device_id_type=MESH)
    send_pre(0)
    loads[3].wait()
    loads[4].wait()
    scaled(gw, gs, gw, DL, HL)
    early = [start_first(q, 0) for q in range(CHUNKS)]
    loads[5].wait()
    loads[6].wait()
    scaled(uw, us, uw, DL, HL)
    pre(1)
    send_pre(1)
    shared = []
    prefetched = []

    def first_steps(q):
        groups = early[q], start_first(q, 1)
        if q == 1:
            prefetched.extend(prefetch())
        return groups

    def do_output(q, arrivals):
        if q == 0:
            copies.arrive(*prefetched)
        entries = output(q, arrivals)
        if q == 1:
            for n in range(CHUNKS):
                start_multipliers(n)
            shared.extend(copies.one(x_ref.at[core, n], x_ref.at[core, n], sibling) for n in range(CHUNKS))
            turned[...] = tok[...].astype(F32).T.astype(BF16)
        return entries

    def do_middle(q, arrivals):
        if q == 0:
            pl.semaphore_wait(ready, 2)
        entries = middle(q, arrivals)
        if q == 1:
            background(BACKGROUND[0])
        return entries

    def do_cotangent(q, arrivals):
        entries = cotangent(q, arrivals)
        if q == 1:
            background(BACKGROUND[1])
        return entries

    def do_spread(q, arrivals):
        group = spread(q, arrivals)
        if q == 1:
            shared.append(share_multipliers(0))
        return group

    def do_backward(q, arrivals):
        entries = backward(q, arrivals)
        if q == 1:
            shared.extend(share_signals(n) for n in range(CHUNKS))
            shared.append(share_multipliers(1))
        return entries

    steps = [activate, do_output, do_middle, do_cotangent, do_spread, do_backward, gradients]
    begun = [first_steps(q) for q in range(CHUNKS)]
    flying = [[], []]
    for p in range(2):
        for q in range(CHUNKS):
            flying[q].append(middle_first(q, p, begun[q][p]))
    for step in steps:
        flying = [step(q, flying[q]) for q in range(CHUNKS)]

    copies.arrive(*shared)
    for q in range(CHUNKS):
        combine(core, q, place)
    down_products()
    copies.sent()
    passed = []
    for near in (1, 0):
        for q in range(CHUNKS):
            origins = [places_from[k] for k in parts[near]]
            copies.arrive(flying[q][near])
            passed.append((q, origins + [place] * near, pass_on(q, origins + [place] * near)))
            for n in origins:
                combine(core, q, n)
    for q, origins, group in passed:
        copies.arrive(group)
        for n in origins:
            combine(1 - core, q, n)
    copies.sent()
    assert len(copies.groups) == GROUPS_SENT


def exchange(*operands):
    vmem = pl.BlockSpec(memory_space=pltpu.VMEM)
    hbm = pl.BlockSpec(memory_space=pltpu.HBM)
    return pl.pallas_call(
        exchange_kernel,
        out_shape=(
            pltpu.VMEM((2, CHUNKS, GROUPS, 32, HL), BF16),
            pltpu.VMEM((HL, DL), F32),
            pltpu.VMEM((HL, DL), F32),
            pltpu.VMEM((DL, 256), BF16),
        ),
        in_specs=[hbm] * 10,
        out_specs=(vmem, vmem, vmem, vmem),
        scratch_shapes=[
            pltpu.VMEM((256, DL), BF16),
            pltpu.VMEM((128, DL), BF16),
            pltpu.VMEM((256, DL), BF16),
            pltpu.VMEM((2, DL, 2 * HL), BF16),
            pltpu.VMEM((HL, DL), BF16),
            pltpu.VMEM((HL, 4 * DL), BF16),
            pltpu.VMEM((DL,), F32),
            pltpu.VMEM((DL,), F32),
            pltpu.VMEM((HL,), F32),
            pltpu.VMEM((CHUNKS, 2, GROUPS, 16, HL), BF16),
            pltpu.VMEM((CHUNKS, 2, GROUPS, 16, HL), BF16),
            pltpu.VMEM((4, 128, HL), F32),
            pltpu.VMEM((CHUNKS, 2, 4, 2, 16, HL), BF16),
            pltpu.VMEM((CHUNKS, 2, 3, 2, 16, HL), BF16),
            pltpu.VMEM((CHUNKS, 2, 4, 16, HL), BF16),
            pltpu.VMEM((CHUNKS, 2, 4, 16, HL), BF16),
            pltpu.VMEM((CHUNKS, 2, 16, HL), F32),
            pltpu.VMEM((2, CHUNKS, GROUPS, 16, HL), BF16),
            pltpu.VMEM((2, CHUNKS, 2, 4, 16, DL), BF16),
            pltpu.VMEM((2, CHUNKS, GROUPS, 16, HL), BF16),
            pltpu.VMEM((2, CHUNKS, GROUPS, 32, HL), BF16),
            pltpu.VMEM((CHUNKS, 2, 2, 4, 16, DL), BF16),
            pltpu.VMEM((CHUNKS, 3, 4, 16, DL), BF16),
            pltpu.VMEM((CHUNKS, 4, 16, DL), BF16),
            pltpu.VMEM((CHUNKS, 3, 16, DL), BF16),
            pltpu.VMEM((CHUNKS, 2, 2, 4, 16, DL), BF16),
            pltpu.VMEM((CHUNKS, GROUPS, 16, HL), BF16),
            pltpu.VMEM((CHUNKS, len(ZERO_STEPS), 16, HL), BF16),
            pltpu.SemaphoreType.DMA((10,)),
            pltpu.SemaphoreType.DMA((SENDS,)),
            pltpu.SemaphoreType.DMA((GROUPS_SENT,)),
            pltpu.SemaphoreType.REGULAR,
        ],
        compiler_params=pltpu.CompilerParams(
            collective_id=0, has_side_effects=True, vmem_limit_bytes=44 * 2**20
        ),
        name="exchange",
    )(*[pltpu.with_memory_space_constraint(operand, pltpu.HBM) for operand in operands])


def products_kernel(turned, g, down, down_tan, gg, ug, dg, gh, uh, dh, square, sems):
    copies = []

    def put(src, out, first, count):
        rows = pl.ds(first, count)
        copy = pltpu.make_async_copy(src.at[rows], out.at[rows], sems.at[len(copies)])
        copy.start()
        copies.append(copy)

    for src, out in ((down, dg), (down_tan, dh)):
        for half in range(2):
            put(src, out, half * (HL // 2), HL // 2)
    for n, out in enumerate((gg, ug, gh, uh)):
        part = g[:, :, :, (n // 2) * 16 : (n // 2) * 16 + 16, :].astype(F32).reshape(32, 2, ROWS, HL)
        rows = part[:, n % 2].reshape(256, HL).astype(BF16)
        for half in range(2):
            first = half * (DL // 2)
            square[n, first : first + DL // 2] = dot(turned[first : first + DL // 2], rows)
            put(square.at[n], out, first, DL // 2)
    for copy in copies:
        copy.wait()


def products(turned, g, down, down_tan):
    vmem = pl.BlockSpec(memory_space=pltpu.VMEM)
    hbm = pl.BlockSpec(memory_space=pl.ANY)
    tall = jax.ShapeDtypeStruct((DL, HL), F32)
    flat = jax.ShapeDtypeStruct((HL, DL), F32)
    return pl.pallas_call(
        products_kernel,
        out_shape=(tall, tall, flat, tall, tall, flat),
        in_specs=[vmem] * 4,
        out_specs=[hbm] * 6,
        scratch_shapes=[pltpu.VMEM((4, DL, HL), F32), pltpu.SemaphoreType.DMA((12,))],
        compiler_params=pltpu.CompilerParams(vmem_limit_bytes=40 * 2**20),
        name="products",
    )(turned, g, down, down_tan)


def local(
    tokens, gate_weight, up_weight, down_weight, gate_scale, up_scale, down_scale, gate_probe, up_probe, down_probe
):
    g, down, down_tan, turned = exchange(
        tokens, gate_weight, up_weight, down_weight, gate_probe, up_probe, down_probe,
        gate_scale, up_scale, down_scale,
    )
    return products(turned, g, down, down_tan)


def solution(mesh):
    in_specs = (
        P(None, "zero"),
        P("zero", "rep"),
        P("zero", "rep"),
        P("rep", "zero"),
        P("zero"),
        P("zero"),
        P("rep"),
        P("zero", "rep"),
        P("zero", "rep"),
        P("rep", "zero"),
    )
    out_specs = (
        P("zero", "rep"),
        P("zero", "rep"),
        P("rep", "zero"),
        P("zero", "rep"),
        P("zero", "rep"),
        P("rep", "zero"),
    )
    return jax.shard_map(local, mesh=mesh, in_specs=in_specs, out_specs=out_specs, check_vma=False)
```

```python
import functools

import jax
import jax.numpy as jnp
from jax import lax
from jax.experimental import pallas as pl
from jax.experimental.pallas import tpu as pltpu
from jax.sharding import PartitionSpec as P

D = 6144
H = 14336
TOKENS = 256

DL = 384
HL = 896
CHUNKS = 2
GROUPS = 8
ROWS = 8
BACKGROUND = (1, 1)
GROUPS_SENT = 49
SENDS = 12

BF16 = jnp.bfloat16
F32 = jnp.float32
MESH = pl.DeviceIdType.MESH

ZERO_STEPS = ((1, 2), (1, 1), (1, 3), (0, 2), (1, 0), (0, 1), (0, 3))
RING_STEPS = (2, 1, 3)


def dot(left, right):
    return jnp.dot(left, right, preferred_element_type=F32)


def dot_last(left, right):
    return lax.dot_general(left, right, (((1,), (1,)), ((), ())), preferred_element_type=F32)


def dot_rows(left, right):
    return lax.dot_general(left, right, (((0,), (0,)), ((), ())), preferred_element_type=F32)


def pair(first, second):
    width = first.shape[-1]
    return jnp.concatenate([first.reshape(-1, ROWS, width), second.reshape(-1, ROWS, width)], axis=1).astype(BF16)


class Copies:
    def __init__(self, send, recv, device):
        self.send, self.recv, self.device = send, recv, device
        self.groups = []
        self.busy = {}

    def start(self, moves, view):
        n = len(self.groups)
        slot = n % SENDS
        if slot in self.busy:
            self.busy.pop(slot).wait_send()
        for src, dst, device in moves:
            pltpu.make_async_remote_copy(
                src_ref=src, dst_ref=dst, send_sem=self.send.at[slot], recv_sem=self.recv.at[n],
                device_id=device, device_id_type=MESH,
            ).start()
        group = pltpu.make_async_remote_copy(
            src_ref=view, dst_ref=view, send_sem=self.send.at[slot], recv_sem=self.recv.at[n],
            device_id=self.device, device_id_type=MESH,
        )
        self.busy[slot] = group
        self.groups.append(group)
        return group

    def one(self, src, dst, device):
        return self.start([(src, dst, device)], dst)

    def arrive(self, *groups):
        for group in groups:
            group.wait_recv()

    def sent(self):
        for slot in list(self.busy):
            self.busy.pop(slot).wait_send()


def exchange_kernel(
    tok_hbm, gw_hbm, uw_hbm, dw_hbm, gp_hbm, up_hbm, dp_hbm, gs_hbm, us_hbm, ds_hbm,
    g_ref, dg_ref, dh_ref, turned,
    tok, tok_sib, tok_order, mats, dw, wide, gs, us, ds,
    sib_out, sib_in, own, stage, far4, near4, sum4, mine4,
    x_ref, y_ref, hids, mult, outs, outs_in, mids, mids_in, back,
    hid, hid_in,
    load_sem, send_sem, recv_sem, ready,
):
    rep = lax.axis_index("rep")
    zero = lax.axis_index("zero")
    core = lax.rem(zero, 2)
    z_lo, x = lax.div(zero, 8), lax.rem(lax.div(zero, 2), 4)
    z_hi, y = lax.div(rep, 4), lax.rem(rep, 4)
    sibling = (rep, zero + 1 - 2 * core)
    twin = (rep, (1 - z_lo) * 8 + x * 2 + core)
    ring_x = [x] + [lax.rem(x + step, 4) for step in (1, 2, 3)]
    xs = [ring_x[step] for step in RING_STEPS]
    ys = [lax.rem(y + step, 4) for step in RING_STEPS]
    zs = [lax.rem(z_hi + step, 4) for step in RING_STEPS]
    x_peers = [(rep, z_lo * 8 + other * 2 + core) for other in xs]
    y_peers = [(z_hi * 4 + other, zero) for other in ys]
    z_peers = [(other * 4 + y, zero) for other in zs]
    ring_z = [z_lo, 1 - z_lo]
    chips = [(ring_x[dx], ring_z[dz]) for dz, dx in ZERO_STEPS]
    chips_from = [(ring_x[(4 - dx) % 4], ring_z[dz]) for dz, dx in ZERO_STEPS]
    places = [2 * other_x + other_z for other_x, other_z in chips]
    places_from = [2 * other_x + other_z for other_x, other_z in chips_from]
    chip_peers = [(rep, other_z * 8 + other_x * 2 + core) for other_x, other_z in chips]
    partners = [sibling, twin] + x_peers + y_peers + z_peers[1:]
    copies = Copies(send_sem, recv_sem, sibling)

    barrier = pltpu.get_barrier_semaphore()
    for other in partners:
        pl.semaphore_signal(barrier, inc=1, device_id=other, device_id_type=MESH)

    gp, up = mats.at[0, :, pl.ds(0, HL)], mats.at[0, :, pl.ds(HL, HL)]
    gw, uw = mats.at[1, :, pl.ds(0, HL)], mats.at[1, :, pl.ds(HL, HL)]
    pairs = (
        (tok_hbm, tok), (gp_hbm, gp), (up_hbm, up), (gs_hbm, gs), (gw_hbm, gw), (us_hbm, us), (uw_hbm, uw),
        (ds_hbm, ds), (dw_hbm, dw), (dp_hbm, wide.at[:, pl.ds(2 * DL, DL)]),
    )
    loads = [pltpu.make_async_copy(src, dst, load_sem.at[n]) for n, (src, dst) in enumerate(pairs)]
    for copy in loads:
        copy.start()

    loads[0].wait()
    tok_order[0:128, :] = tok[pl.ds(pl.multiple_of((1 - core) * 128, 128), 128), :]
    tok_order[128:256, :] = tok[pl.ds(pl.multiple_of(core * 128, 128), 128), :]
    tokens = tok_order[...]

    def scaled(ref, scale_ref, out_ref, rows, width):
        column = jnp.broadcast_to(scale_ref[...].reshape(1, rows), (128, rows)).T
        for n in range(width // 128):
            block = slice(n * 128, (n + 1) * 128)
            out_ref[:, block] = (ref[:, block].astype(F32) * column).astype(BF16)

    from_sib = {}

    def pre(p):
        wide_result = dot(tokens, mats[p])
        a, b = wide_result[:, 0:HL], wide_result[:, HL : 2 * HL]
        own[2 * p] = a[128:256]
        own[2 * p + 1] = b[128:256]
        both = pair(a[0:128], b[0:128])
        for q in range(CHUNKS):
            sib_out[q, p] = both[q * GROUPS : (q + 1) * GROUPS]

    def send_pre(p):
        for q in range(CHUNKS):
            from_sib[q, p] = copies.one(sib_out.at[q, p], sib_in.at[q, p], sibling)

    def sum_start(q, parts, far, near):
        if q == 0:
            return copies.start([(parts.at[other], far.at[k], x_peers[k]) for k, other in enumerate(xs)], far)
        return copies.one(parts.at[:, 1 - z_lo], near, twin)

    def sum_middle(q, parts, far, near, out, mine, ours, arrival):
        copies.arrive(arrival)
        if q == 0:
            total = ours
            for k in range(3):
                total = total + far[k].astype(F32)
            mine[...] = jnp.where(z_lo == 0, total[0], total[1])
            out[0] = jnp.where(z_lo == 0, total[1], total[0]).astype(BF16)
            return copies.one(out.at[0], near.at[0], twin)
        out[...] = (parts[:, z_lo].astype(F32) + near[...].astype(F32)).astype(BF16)
        group = copies.start(
            [(out.at[other], far.at[k, 0], x_peers[k]) for k, other in enumerate(xs)], far.at[:, 0]
        )
        mine[...] = ours + near[x].astype(F32)
        return group

    def sum_end(q, far, near, mine, arrival):
        copies.arrive(arrival)
        total = mine[...]
        if q == 0:
            return total + near[0].astype(F32)
        for k in range(3):
            total = total + far[k, 0].astype(F32)
        return total

    place = 2 * x + z_lo

    def gather(blocks, steps):
        block = blocks.at[place]
        return copies.start([(block, block, chip_peers[k]) for k in steps], blocks.at[pl.ds(0, len(steps))])

    feature_factor = float(D) ** -0.5
    hidden_factor = float(H) ** -0.5
    factor = float(TOKENS) ** -0.5

    def start_first(q, p):
        copies.arrive(from_sib[q, p])
        a = own[2 * p, q * 64 : (q + 1) * 64].reshape(GROUPS, ROWS, HL)
        b = own[2 * p + 1, q * 64 : (q + 1) * 64].reshape(GROUPS, ROWS, HL)
        both = (jnp.concatenate([a, b], axis=1) + sib_in[q, p].astype(F32)).astype(BF16)
        stage[q, p] = both.reshape(4, 2, 16, HL)
        return sum_start(q, stage.at[q, p], far4.at[q, p], near4.at[q, p])

    def middle_first(q, p, arrivals):
        count = 2 if q == 0 else 1
        group = x * 2 if q == 0 else x * 2 + z_lo
        rows = pl.ds(pl.multiple_of(q * 64 + group * ROWS, ROWS), count * ROWS)
        kept = [own[2 * p + n, rows, :].reshape(count, ROWS, HL) for n in range(2)]
        ours = jnp.concatenate(kept, axis=1) + sib_in[q, p, pl.ds(group, count)].astype(F32)
        if q == 1:
            ours = ours[0]
        return sum_middle(
            q, stage.at[q, p], far4.at[q, p], near4.at[q, p], sum4.at[q, p], mine4.at[q, p], ours, arrivals
        )

    multipliers = []

    def activate(q, arrivals):
        totals = [
            sum_end(q, far4.at[q, p], near4.at[q, p], mine4.at[q, p], arrivals[p]) for p in range(2)
        ]
        gate_tan, up_tan, gate_pre, up_pre = [total[n : n + ROWS] for total in totals for n in (0, ROWS)]
        gate_tan = feature_factor * gate_tan
        up_tan = feature_factor * up_tan
        logistic = jax.nn.sigmoid(gate_pre)
        act = gate_pre * logistic
        slope = logistic * (1.0 + gate_pre * (1.0 - logistic))
        bend = logistic * (1.0 - logistic) * (2.0 + gate_pre * (1.0 - 2.0 * logistic))
        lean = slope * gate_tan
        x_ref[core, q, place] = jnp.concatenate([act * up_pre, lean * up_pre + act * up_tan], axis=0).astype(BF16)
        group = gather(x_ref.at[core, q], range(len(chips)))
        mult[core, q, place] = jnp.concatenate(
            [up_pre * slope, act, up_tan * slope + up_pre * bend * gate_tan, lean], axis=0
        ).astype(BF16)
        return group

    def start_multipliers(q):
        block = mult.at[core, q, place]
        multipliers.append(copies.one(block, block, twin))

    waiting = list(range(CHUNKS))

    def background(count):
        for q in waiting[:count]:
            copies.arrive(multipliers[q])
            block = mult.at[core, q, pl.ds(2 * x, 2)]
            multipliers[q] = copies.start([(block, block, peer) for peer in x_peers], mult.at[core, q, pl.ds(0, 6)])
        del waiting[:count]

    def share_multipliers(q):
        copies.arrive(multipliers[q])
        return copies.one(mult.at[core, q], mult.at[core, q], sibling)

    def output(q, arrival):
        copies.arrive(arrival)
        hidden = x_ref[core, q].reshape(GROUPS * 16, HL)
        result = dot(hidden, wide[...])
        for f in range(2):
            straight = result[:, f * DL : (f + 1) * DL].reshape(GROUPS, 2, ROWS, DL)
            probed = result[:, (f + 2) * DL : (f + 3) * DL].reshape(GROUPS, 2, ROWS, DL)
            outs[q, f] = jnp.concatenate(
                [straight[:, 0], hidden_factor * probed[:, 0] + straight[:, 1]], axis=1
            ).astype(BF16).reshape(2, 4, 16, DL)
        group = copies.start(
            [(outs.at[q, lax.rem(other, 2), lax.div(other, 2)], outs_in.at[q, k], y_peers[k]) for k, other in enumerate(ys)],
            outs_in.at[q],
        )
        return group

    half, high = lax.rem(y, 2), lax.div(y, 2)

    def middle(q, arrival):
        copies.arrive(arrival)
        total = outs[q, half, high].astype(F32)
        for k in range(3):
            total += outs_in[q, k].astype(F32)
        mids[q] = total.astype(BF16)
        return copies.start(
            [(mids.at[q, other], mids_in.at[q, k], z_peers[k]) for k, other in enumerate(zs)], mids_in.at[q]
        )

    def cotangent(q, arrival):
        copies.arrive(arrival)
        total = mids[q, z_hi].astype(F32)
        for k in range(3):
            total += mids_in[q, k].astype(F32)
        row = pl.multiple_of(q * 64 + high * 32 + lax.div(z_hi, 2) * 16, 16)
        own_tokens = tok[pl.ds(pl.multiple_of(core * 128 + row, 16), 16), :].astype(F32)
        sib_tokens = tok_sib[pl.ds(row, 16), :].astype(F32)
        chosen = jnp.where(half == 0, own_tokens, sib_tokens)
        chosen = jnp.where(lax.rem(z_hi, 2) == 0, chosen[0:8], chosen[8:16])
        back[q, half, high, z_hi] = jnp.concatenate(
            [factor * (chosen + total[0:8]), factor * total[8:16]], axis=0
        ).astype(BF16)
        block = back.at[q, half, high, z_hi]
        return copies.start([(block, block, peer) for peer in z_peers], back.at[q, half, high, pl.ds(0, 3)])

    def spread(q, arrival):
        copies.arrive(arrival)
        block = back.at[q, half, high]
        return copies.start([(block, block, peer) for peer in y_peers], outs_in.at[q])

    def backward(q, arrival):
        copies.arrive(arrival)
        signals = jnp.concatenate([back[q, f].reshape(GROUPS * 16, DL) for f in range(2)], axis=1)
        straight = dot_last(signals, wide[:, 0 : 2 * DL]).reshape(GROUPS, 2, ROWS, HL)
        probed = dot_last(signals, wide[:, 2 * DL : 4 * DL]).reshape(GROUPS, 2, ROWS, HL)
        both = jnp.concatenate([straight[:, 0], straight[:, 1] + hidden_factor * probed[:, 0]], axis=1)
        hid[q] = both.astype(BF16)
        group = copies.start(
            [(hid.at[q, other], hid_in.at[q, k], chip_peers[k]) for k, other in enumerate(places)], hid_in.at[q]
        )
        return group

    def share_signals(q):
        y_ref[core, q] = back[q, 0]
        return copies.one(back.at[q, 1], y_ref.at[core, q], sibling)

    parts = (range(0, 2), range(2, 4), range(4, 7))

    def pass_on(q, origins):
        blocks = [hids.at[core, q, n] for n in origins]
        return copies.start([(block, block, sibling) for block in blocks], hids.at[core, q, pl.ds(0, len(blocks))])

    def gradients(q, arrival):
        copies.arrive(arrival)
        total = hid[q, place].astype(F32)
        for k in range(len(chips)):
            total += hid_in[q, k].astype(F32)
        hids[core, q, place] = total.astype(BF16)
        return [gather(hids.at[core, q], steps) for steps in parts]

    def combine(side, q, n):
        signals = hids[side, q, n].astype(F32)
        signal, signal_tan = signals[0:8], signals[8:16]
        factors = mult[side, q, n].astype(F32)
        first, second, third, fourth = [factors[m * ROWS : (m + 1) * ROWS] for m in range(4)]
        g_ref[side, q, n] = jnp.concatenate(
            [
                signal * first,
                signal * second,
                signal_tan * first + signal * third,
                signal_tan * second + signal * fourth,
            ],
            axis=0,
        ).astype(BF16)

    def down_products():
        hidden = x_ref[...].reshape(512, HL)
        signals = y_ref[...].astype(F32).reshape(32, 2, ROWS, DL)
        straight = jnp.concatenate([signals[:, 0], jnp.zeros_like(signals[:, 0])], axis=1)
        swapped = jnp.concatenate([signals[:, 1], signals[:, 0]], axis=1)
        dg_ref[...] = dot_rows(hidden, straight.astype(BF16).reshape(512, DL))
        dh_ref[...] = dot_rows(hidden, swapped.astype(BF16).reshape(512, DL))

    def prefetch():
        loads[7].wait()
        loads[8].wait()
        scaled(dw, ds, wide.at[:, pl.ds(0, DL)], HL, DL)
        loads[9].wait()
        theirs = tok.at[pl.ds(pl.multiple_of((1 - core) * 128, 128), 128)]
        return [
            copies.one(wide.at[:, pl.ds(0, DL)], wide.at[:, pl.ds(DL, DL)], sibling),
            copies.one(wide.at[:, pl.ds(2 * DL, DL)], wide.at[:, pl.ds(3 * DL, DL)], sibling),
            copies.one(theirs, tok_sib, sibling),
        ]

    loads[1].wait()
    loads[2].wait()
    pre(0)
    pl.semaphore_wait(barrier, len(partners))
    for other in z_peers[1:]:
        pl.semaphore_signal(ready, inc=1, device_id=other, device_id_type=MESH)
    send_pre(0)
    loads[3].wait()
    loads[4].wait()
    scaled(gw, gs, gw, DL, HL)
    early = [start_first(q, 0) for q in range(CHUNKS)]
    loads[5].wait()
    loads[6].wait()
    scaled(uw, us, uw, DL, HL)
    pre(1)
    send_pre(1)
    shared = []
    prefetched = []

    def first_steps(q):
        groups = early[q], start_first(q, 1)
        if q == 1:
            prefetched.extend(prefetch())
        return groups

    def do_output(q, arrivals):
        if q == 0:
            copies.arrive(*prefetched)
        entries = output(q, arrivals)
        if q == 1:
            for n in range(CHUNKS):
                start_multipliers(n)
            shared.extend(copies.one(x_ref.at[core, n], x_ref.at[core, n], sibling) for n in range(CHUNKS))
            turned[...] = tok[...].astype(F32).T.astype(BF16)
        return entries

    def do_middle(q, arrivals):
        if q == 0:
            pl.semaphore_wait(ready, 2)
        entries = middle(q, arrivals)
        if q == 1:
            background(BACKGROUND[0])
        return entries

    def do_cotangent(q, arrivals):
        entries = cotangent(q, arrivals)
        if q == 1:
            background(BACKGROUND[1])
        return entries

    def do_spread(q, arrivals):
        group = spread(q, arrivals)
        if q == 1:
            shared.append(share_multipliers(0))
        return group

    def do_backward(q, arrivals):
        entries = backward(q, arrivals)
        if q == 1:
            shared.extend(share_signals(n) for n in range(CHUNKS))
            shared.append(share_multipliers(1))
        return entries

    steps = [activate, do_output, do_middle, do_cotangent, do_spread, do_backward, gradients]
    begun = [first_steps(q) for q in range(CHUNKS)]
    flying = [[], []]
    for p in range(2):
        for q in range(CHUNKS):
            flying[q].append(middle_first(q, p, begun[q][p]))
    for step in steps:
        flying = [step(q, flying[q]) for q in range(CHUNKS)]

    copies.arrive(*shared)
    for q in range(CHUNKS):
        combine(core, q, place)
    down_products()
    copies.sent()
    passed = []
    for near in (2, 1, 0):
        for q in range(CHUNKS):
            origins = [places_from[k] for k in parts[near]]
            copies.arrive(flying[q][near])
            passed.append((q, origins + [place] * (near == 2), pass_on(q, origins + [place] * (near == 2))))
            for n in origins:
                combine(core, q, n)
    for q, origins, group in passed:
        copies.arrive(group)
        for n in origins:
            combine(1 - core, q, n)
    copies.sent()
    assert len(copies.groups) == GROUPS_SENT


def exchange(*operands):
    vmem = pl.BlockSpec(memory_space=pltpu.VMEM)
    hbm = pl.BlockSpec(memory_space=pltpu.HBM)
    return pl.pallas_call(
        exchange_kernel,
        out_shape=(
            pltpu.VMEM((2, CHUNKS, GROUPS, 32, HL), BF16),
            pltpu.VMEM((HL, DL), F32),
            pltpu.VMEM((HL, DL), F32),
            pltpu.VMEM((DL, 256), BF16),
        ),
        in_specs=[hbm] * 10,
        out_specs=(vmem, vmem, vmem, vmem),
        scratch_shapes=[
            pltpu.VMEM((256, DL), BF16),
            pltpu.VMEM((128, DL), BF16),
            pltpu.VMEM((256, DL), BF16),
            pltpu.VMEM((2, DL, 2 * HL), BF16),
            pltpu.VMEM((HL, DL), BF16),
            pltpu.VMEM((HL, 4 * DL), BF16),
            pltpu.VMEM((DL,), F32),
            pltpu.VMEM((DL,), F32),
            pltpu.VMEM((HL,), F32),
            pltpu.VMEM((CHUNKS, 2, GROUPS, 16, HL), BF16),
            pltpu.VMEM((CHUNKS, 2, GROUPS, 16, HL), BF16),
            pltpu.VMEM((4, 128, HL), F32),
            pltpu.VMEM((CHUNKS, 2, 4, 2, 16, HL), BF16),
            pltpu.VMEM((CHUNKS, 2, 3, 2, 16, HL), BF16),
            pltpu.VMEM((CHUNKS, 2, 4, 16, HL), BF16),
            pltpu.VMEM((CHUNKS, 2, 4, 16, HL), BF16),
            pltpu.VMEM((CHUNKS, 2, 16, HL), F32),
            pltpu.VMEM((2, CHUNKS, GROUPS, 16, HL), BF16),
            pltpu.VMEM((2, CHUNKS, 2, 4, 16, DL), BF16),
            pltpu.VMEM((2, CHUNKS, GROUPS, 16, HL), BF16),
            pltpu.VMEM((2, CHUNKS, GROUPS, 32, HL), BF16),
            pltpu.VMEM((CHUNKS, 2, 2, 4, 16, DL), BF16),
            pltpu.VMEM((CHUNKS, 3, 4, 16, DL), BF16),
            pltpu.VMEM((CHUNKS, 4, 16, DL), BF16),
            pltpu.VMEM((CHUNKS, 3, 16, DL), BF16),
            pltpu.VMEM((CHUNKS, 2, 2, 4, 16, DL), BF16),
            pltpu.VMEM((CHUNKS, GROUPS, 16, HL), BF16),
            pltpu.VMEM((CHUNKS, len(ZERO_STEPS), 16, HL), BF16),
            pltpu.SemaphoreType.DMA((10,)),
            pltpu.SemaphoreType.DMA((SENDS,)),
            pltpu.SemaphoreType.DMA((GROUPS_SENT,)),
            pltpu.SemaphoreType.REGULAR,
        ],
        compiler_params=pltpu.CompilerParams(
            collective_id=0, has_side_effects=True, vmem_limit_bytes=44 * 2**20
        ),
        name="exchange",
    )(*[pltpu.with_memory_space_constraint(operand, pltpu.HBM) for operand in operands])


def products_kernel(turned, g, down, down_tan, gg, ug, dg, gh, uh, dh, square, sems):
    copies = []

    def put(src, out, first, count):
        rows = pl.ds(first, count)
        copy = pltpu.make_async_copy(src.at[rows], out.at[rows], sems.at[len(copies)])
        copy.start()
        copies.append(copy)

    for src, out in ((down, dg), (down_tan, dh)):
        for half in range(2):
            put(src, out, half * (HL // 2), HL // 2)
    for n, out in enumerate((gg, ug, gh, uh)):
        part = g[:, :, :, (n // 2) * 16 : (n // 2) * 16 + 16, :].astype(F32).reshape(32, 2, ROWS, HL)
        rows = part[:, n % 2].reshape(256, HL).astype(BF16)
        for half in range(2):
            first = half * (DL // 2)
            square[n, first : first + DL // 2] = dot(turned[first : first + DL // 2], rows)
            put(square.at[n], out, first, DL // 2)
    for copy in copies:
        copy.wait()


def products(turned, g, down, down_tan):
    vmem = pl.BlockSpec(memory_space=pltpu.VMEM)
    hbm = pl.BlockSpec(memory_space=pl.ANY)
    tall = jax.ShapeDtypeStruct((DL, HL), F32)
    flat = jax.ShapeDtypeStruct((HL, DL), F32)
    return pl.pallas_call(
        products_kernel,
        out_shape=(tall, tall, flat, tall, tall, flat),
        in_specs=[vmem] * 4,
        out_specs=[hbm] * 6,
        scratch_shapes=[pltpu.VMEM((4, DL, HL), F32), pltpu.SemaphoreType.DMA((12,))],
        compiler_params=pltpu.CompilerParams(vmem_limit_bytes=40 * 2**20),
        name="products",
    )(turned, g, down, down_tan)


def local(
    tokens, gate_weight, up_weight, down_weight, gate_scale, up_scale, down_scale, gate_probe, up_probe, down_probe
):
    g, down, down_tan, turned = exchange(
        tokens, gate_weight, up_weight, down_weight, gate_probe, up_probe, down_probe,
        gate_scale, up_scale, down_scale,
    )
    return products(turned, g, down, down_tan)


def solution(mesh):
    in_specs = (
        P(None, "zero"),
        P("zero", "rep"),
        P("zero", "rep"),
        P("rep", "zero"),
        P("zero"),
        P("zero"),
        P("rep"),
        P("zero", "rep"),
        P("zero", "rep"),
        P("rep", "zero"),
    )
    out_specs = (
        P("zero", "rep"),
        P("zero", "rep"),
        P("rep", "zero"),
        P("zero", "rep"),
        P("zero", "rep"),
        P("rep", "zero"),
    )
    return jax.shard_map(local, mesh=mesh, in_specs=in_specs, out_specs=out_specs, check_vma=False)
```
